32 devices in a mesh: slab: 8 (over y, x, core), buddy: 4 (over z).
Axes of the slice: x: 2, y: 2, z: 4, core: 2. Of those that a mesh axis runs over, the one named last changes fastest.
Arguments:
- checkpoint: float32 [32, 5, 64, 4, 256], P('buddy', None, 'slab'), may hold values from -6 to 6
- slot_block: int32 [4, 8], replicated, may hold values from 0 to 31, as said below
- live_state: float32 [4, 5, 64, 32, 256], P('buddy', None, 'slab'), may hold values from -6 to 6
- levels: int32 [2, 4, 3], P(None, 'buddy'), may hold values from 0 to 2
- coefficients: float32 [2, 4], P(None, 'buddy'), may hold values from 0.3 to 1
- tile_owner: int32 [8, 16], P('slab'), may hold values from 0 to 3, as said below
Outputs:
- recovered: float32 [4, 5, 64, 32, 256], P('buddy', None, 'slab')
- combined: float32 [32, 5, 64, 2, 256], P('buddy', None, 'slab')
The draws below stay inside these ranges and needn't reach their ends.
Inputs may be any that keep to these rules, and one draw needn't show every extreme that they name: `slot_block`: row h lists the blocks in the 8 slots of holder h, block j of grid g written g * 8 + j. Every block is held exactly once, never by its own grid's holder; one holder keeps at most 3 blocks of one grid, and some holder keeps exactly 3 of some grid. `tile_owner`: no reader reads more than 8 tiles of one slab, and in every slab some reader reads exactly 8.
All inputs are finite; a program needn't handle non-finite values.
Results may differ from the reference program's by a relative error of at most 0.000096.
Values sent between devices are 32-bit elements; how exact they have to be, the bound alone decides.
No kernel may reach another device: no remote copies, remote signals or barrier semaphores. Data moves between devices by JAX's collectives and lax.ppermute only.
A program may use at most 192 MiB of HBM per device.

```python
import jax
import jax.numpy as jnp

CX = 256
CY = 32
CZ = 8
BLOCKS = 8
HELD_MOST = 3
TILE_LINES = 2
GRIDS = 4
SLABS = 8
NZ = 64
BLOCK_LINES = 4
TILES = 16
READ_MOST = 8


def draw_slot_block(key, part):
    key_place, key_offset, key_slots, key_blocks = jax.random.split(key, 4)
    placing = jax.random.permutation(key_place, GRIDS).astype(jnp.int32)
    position = jnp.zeros((GRIDS,), jnp.int32).at[placing].set(jnp.arange(GRIDS, dtype=jnp.int32))
    offset = jax.random.randint(key_offset, (), 0, GRIDS - 1).astype(jnp.int32)
    shift_group = jax.vmap(lambda sub_key: jax.random.permutation(sub_key, BLOCKS))(jax.random.split(key_slots, GRIDS)).astype(jnp.int32)
    block_order = jax.vmap(lambda sub_key: jax.random.permutation(sub_key, BLOCKS))(jax.random.split(key_blocks, GRIDS)).astype(jnp.int32)
    shifts = 1 + (shift_group // HELD_MOST + offset) % (GRIDS - 1)
    owners = placing[(position[:, None] - shifts) % GRIDS]
    chosen_blocks = block_order[owners, shift_group]
    return (owners * BLOCKS + chosen_blocks).astype(jnp.int32)


def draw_tile_owner(key, part):

    def one_slab(slab_key):
        key_tiles, key_readers = jax.random.split(slab_key)
        tile_order = jax.random.permutation(key_tiles, TILES).astype(jnp.int32)
        readers = jax.random.permutation(key_readers, GRIDS).astype(jnp.int32)
        counter = jnp.arange(TILES, dtype=jnp.int32)
        others = (counter - READ_MOST) % (GRIDS - 1) + 1
        chosen = jnp.where(counter < READ_MOST, readers[0], readers[others])
        return jnp.zeros((TILES,), jnp.int32).at[tile_order].set(chosen.astype(jnp.int32))
    return jax.vmap(one_slab)(jax.random.split(key, SLABS))


def plant(drawn, own_key, least, largest):
    extent = drawn.shape
    spot = [jax.random.randint(jax.random.fold_in(own_key, axis), (), 0, extent[axis]) for axis in range(len(extent))]
    drawn = drawn.at[tuple(spot)].set(least)
    longest = extent.index(max(extent))
    spot[longest] = (spot[longest] + 1) % extent[longest]
    return drawn.at[tuple(spot)].set(largest)


def block_levels(stream_key, dims, cuts, low, top_value):
    factor_of, own = 1.0, jax.random.fold_in(stream_key, 6)
    for axis_at, parts in cuts:
        steps = jnp.exp(jax.random.uniform(jax.random.fold_in(own, axis_at), (parts,), jnp.float32, low / len(cuts), top_value / len(cuts)))
        factor_of = factor_of * jnp.repeat(steps, dims[axis_at] // parts).reshape([-1 if axis == axis_at else 1 for axis in range(len(dims))])
    return factor_of


def gaussian(stream_key, shape, deviation, limit, cuts=(), kind=jnp.bfloat16):
    entries = jax.random.normal(stream_key, shape, jnp.float32) * deviation
    if len(cuts) > 0:
        entries = block_levels(stream_key, shape, cuts, -0.22, 0.18) * entries
    return jnp.clip(entries, min=-limit, max=limit).astype(kind)


def setup_inputs(seed: int = 0) -> dict:
    key_of = jax.random.split(jax.random.key(seed), 7)
    checkpoint = gaussian(key_of[0], (GRIDS * BLOCKS, 5, NZ, BLOCK_LINES, CX), 1.0, 6.0, ((0, 4), (2, 8)), jnp.float32)
    slot_block = draw_slot_block(jax.random.fold_in(key_of[6], 71), 0)
    live_state = gaussian(key_of[2], (GRIDS, 5, NZ, CY, CX), 1.0, 6.0, ((0, 4), (2, 8)), jnp.float32)
    levels = plant(jax.random.randint(key_of[3], (2, GRIDS, 3), 0, 3), jax.random.fold_in(key_of[3], 1), 0, 2).astype(jnp.int32)
    coefficients = jnp.clip(0.3 + 0.7 * jax.random.uniform(key_of[4], (2, GRIDS), jnp.float32) ** block_levels(key_of[4], (2, GRIDS), ((1, 4),), -0.2, 0.2), 0.3, 1.0)
    tile_owner = draw_tile_owner(jax.random.fold_in(key_of[6], 71), 0)
    return {"checkpoint": checkpoint, "slot_block": slot_block, "live_state": live_state, "levels": levels, "coefficients": coefficients, "tile_owner": tile_owner}


VELOCITY = (0.3, -0.2, 0.45)
COURANT = 1.0


def apply_matrix(difference, axis_number):
    drift_speed = VELOCITY[axis_number]
    channels = [difference[..., channel_index, :, :, :] for channel_index in range(5)]
    pressure = channels[4]
    normal_velocity = channels[1 + axis_number]
    result = [drift_speed * channels[0] + normal_velocity, drift_speed * channels[1], drift_speed * channels[2], drift_speed * channels[3], drift_speed * pressure + normal_velocity]
    result[1 + axis_number] = result[1 + axis_number] + pressure
    return jnp.stack(result, axis=-4)


def direction_rate(plus_side, minus_side, middle, inv_spacing, axis_number):
    wave_speed = abs(VELOCITY[axis_number]) + 1.0
    flux_term = apply_matrix(plus_side - minus_side, axis_number)
    return inv_spacing * (0.5 * flux_term - (0.5 * wave_speed) * (plus_side + minus_side - 2.0 * middle))


def section_rate(padded, inv_spacing):
    middle = padded[..., 1:-1, :, :]
    summed_rate = direction_rate(jnp.roll(middle, -1, -1), jnp.roll(middle, 1, -1), middle, inv_spacing[0], 0)
    summed_rate = summed_rate + direction_rate(jnp.roll(middle, -1, -2), jnp.roll(middle, 1, -2), middle, inv_spacing[1], 1)
    summed_rate = summed_rate + direction_rate(padded[..., 2:, :, :], padded[..., :-2, :, :], middle, inv_spacing[2], 2)
    return -summed_rate


def spacing_terms(level_rows):
    inverse = jnp.exp2(level_rows.astype(jnp.float32))
    count_rows = level_rows.shape[0]
    members = tuple(inverse[:, axis_number].reshape(count_rows, 1, 1, 1, 1) for axis_number in range(3))
    denominator = (abs(VELOCITY[0]) + 1.0) * members[0] + (abs(VELOCITY[1]) + 1.0) * members[1]
    denominator = denominator + (abs(VELOCITY[2]) + 1.0) * members[2]
    return members, COURANT / denominator


def advance(state, inv_spacing, time_step, widen):
    first_rate = section_rate(widen(state), inv_spacing)
    second_rate = section_rate(widen(state + (0.5 * time_step) * first_rate), inv_spacing)
    third_rate = section_rate(widen(state + (0.5 * time_step) * second_rate), inv_spacing)
    fourth_rate = section_rate(widen(state + time_step * third_rate), inv_spacing)
    return state + (time_step / 6.0) * (first_rate + 2.0 * second_rate + 2.0 * third_rate + fourth_rate)


def wrap_layers(state):
    return jnp.concatenate([state[:, :, -1:], state, state[:, :, :1]], axis=2)


def reference(checkpoint, slot_block, live_state, levels, coefficients, tile_owner):
    flat_ids = slot_block.reshape(-1).astype(jnp.int32)
    ordered = jnp.zeros_like(checkpoint).at[flat_ids].set(checkpoint)
    restored = ordered.reshape(GRIDS, BLOCKS, 5, NZ, BLOCK_LINES, CX).transpose(0, 2, 3, 1, 4, 5).reshape(GRIDS, 5, NZ, CY, CX)
    lost_spacing, lost_step = spacing_terms(levels[0])
    live_spacing, live_step = spacing_terms(levels[1])
    recovered = advance(restored, lost_spacing, lost_step, wrap_layers)
    advanced = advance(live_state, live_spacing, live_step, wrap_layers)
    weighted = coefficients[0].reshape(GRIDS, 1, 1, 1, 1) * recovered + coefficients[1].reshape(GRIDS, 1, 1, 1, 1) * advanced
    summed = jnp.sum(weighted, axis=0)
    tiles = summed.reshape(5, SLABS, CZ, TILES, TILE_LINES, CX).transpose(1, 3, 0, 2, 4, 5)
    hits = (tile_owner[:, :, None] == jnp.arange(GRIDS, dtype=jnp.int32)[None, None, :]).astype(jnp.int32)
    before = jnp.cumsum(hits, axis=1) - hits
    ranks = jnp.sum(before * hits, axis=2).astype(jnp.int32)
    slab_index = jnp.broadcast_to(jnp.arange(SLABS, dtype=jnp.int32)[:, None], (SLABS, TILES))
    placed = jnp.zeros((GRIDS, READ_MOST, SLABS, 5, CZ, TILE_LINES, CX), summed.dtype)
    placed = placed.at[tile_owner.astype(jnp.int32), ranks, slab_index].set(tiles)
    combined = placed.transpose(0, 1, 3, 2, 4, 5, 6).reshape(GRIDS * READ_MOST, 5, SLABS * CZ, TILE_LINES, CX)
    return recovered, combined
```

```python
import functools

import jax
import jax.numpy as jnp
from jax import lax
from jax.experimental import pallas as pl
from jax.experimental.pallas import tpu as pltpu
from jax.sharding import PartitionSpec as P

VELOCITY = (0.3, -0.2, 0.45)
COURANT = 1.0
TILE_LINES = 2
HELD_MOST = 3
DEPTH = 4
LANES = 128
ROWS = 8
VMEM_BYTES = 48 * 1024 * 1024


def spec_vmem():
    return pl.BlockSpec(memory_space=pltpu.VMEM)


def spec_smem():
    return pl.BlockSpec(memory_space=pltpu.SMEM)


def spec_any():
    return pl.BlockSpec(memory_space=pl.ANY)


def params():
    return pltpu.CompilerParams(vmem_limit_bytes=VMEM_BYTES)


def shape(*dims):
    return jax.ShapeDtypeStruct(dims, jnp.float32)


def add(*terms):
    total = None
    for term in terms:
        if term is not None:
            total = term if total is None else total + term
    return total


def sub(left, right):
    if right is None:
        return left
    return -right if left is None else left - right


def mul(factor, term):
    return None if term is None else factor * term


def lane_index():
    return lax.broadcasted_iota(jnp.int32, (ROWS, LANES), 1)


def turn_lanes(value, amount):
    return None if value is None else pltpu.roll(value, amount, 1)


def split_parity(left, right):
    lane = lane_index()
    even_at = (2 * lane) % LANES
    first = lane < LANES // 2
    pick = lambda array, at: jnp.take_along_axis(array, at, axis=1)
    even = jnp.where(first, pick(left, even_at), pick(right, even_at))
    odd = jnp.where(first, pick(left, even_at + 1), pick(right, even_at + 1))
    return even, odd


def join_parity(even, odd):
    lane = lane_index()
    half = lane // 2
    is_even = lane % 2 == 0
    pick = lambda array, at: jnp.take_along_axis(array, at, axis=1)
    left = jnp.where(is_even, pick(even, half), pick(odd, half))
    right = jnp.where(is_even, pick(even, half + LANES // 2), pick(odd, half + LANES // 2))
    return left, right


def pick_rows(array, at):
    return jnp.take_along_axis(array, at, axis=0)


def direction_factors(axis_number):
    drift = VELOCITY[axis_number]
    wave = abs(drift) + 1.0
    carried = (0.5 * (wave - drift), 0.5 * (wave + drift))
    if drift >= 0:
        rising = (0.0, 0.5 * wave)
        falling = (0.5, 0.5 * drift)
    else:
        rising = (-0.5 * drift, 0.5)
        falling = (0.5 * wave, 0.0)
    return carried, rising, falling


def factor_table(spacing, time_step, weight):
    sections = []
    for number, part in enumerate((4.0, 3.0, 2.0, 1.0)):
        scale = time_step / part
        if number == 3:
            scale = scale * weight
        rows = []
        centre = 0.0
        for axis_number in range(3):
            unit = scale * spacing[axis_number]
            centre = centre - unit * (abs(VELOCITY[axis_number]) + 1.0)
            carried, rising, falling = direction_factors(axis_number)
            one_sided = rising if 0.0 in rising else falling
            two_sided = falling if 0.0 in rising else rising
            rows += [
                unit * carried[0],
                unit * carried[1],
                unit * (one_sided[0] + one_sided[1]),
                unit * two_sided[0],
                unit * two_sided[1],
            ]
        sections.append(jnp.stack([centre] + rows + [weight * jnp.ones_like(scale)]))
    return jnp.stack(sections)


def acoustic(axis_number, factors, rising_next, rising_prev, falling_next, falling_prev):
    one, two_next, two_prev = factors
    if VELOCITY[axis_number] >= 0:
        rising = mul(one, rising_prev)
        falling = add(mul(two_next, falling_next), mul(two_prev, falling_prev))
    else:
        rising = add(mul(two_next, rising_next), mul(two_prev, rising_prev))
        falling = mul(one, falling_next)
    return add(rising, falling), sub(rising, falling)


def section(src, src_lines, src_at, state, state_at, dst, dst_lines, dst_at, count, factors, wrap, scaled):
    def layer(number, carry):
        cache = {}

        def cell(field, parity, line, step=0):
            low, high = src_lines
            key = (field, parity, line, step)
            if key in cache:
                return cache[key]
            if low <= line < high:
                value = src[field, src_at + number + step, parity, line - low]
            elif wrap and line < low:
                value = pltpu.roll(cell(field, parity, high - 1), 1, 0)
            elif wrap:
                value = pltpu.roll(cell(field, parity, low), ROWS - 1, 0)
            else:
                value = None
            cache[key] = value
            return value

        def pair(axis_number, parity, line, step=0):
            key = ("pair", axis_number, parity, line, step)
            if key not in cache:
                pressure = cell(4, parity, line, step)
                speed = cell(1 + axis_number, parity, line, step)
                cache[key] = (None, None) if pressure is None else (pressure + speed, pressure - speed)
            return cache[key]

        centre = factors[0]
        for line in range(*dst_lines):
            for parity in (0, 1):
                result = [None] * 5
                for field in range(5):
                    terms = mul(centre, cell(field, parity, line))
                    if 0 <= line < 4:
                        held = state[field, state_at + number, parity, line]
                        terms = add(mul(factors[16], held) if scaled else held, terms)
                    result[field] = terms
                for axis_number in range(3):
                    forward, backward, *sound = factors[1 + 5 * axis_number : 6 + 5 * axis_number]

                    def neighbours(read):
                        if axis_number == 0:
                            other = read(1 - parity, line, 0)
                            if parity == 0:
                                return other, [turn_lanes(part, 1) for part in other]
                            return [turn_lanes(part, LANES - 1) for part in other], other
                        if axis_number == 1:
                            return read(parity, line + 1, 0), read(parity, line - 1, 0)
                        return read(parity, line, 1), read(parity, line, -1)

                    for field in range(4):
                        if field != 1 + axis_number:
                            (after,), (before,) = neighbours(
                                lambda *where, field=field: [cell(field, *where)]
                            )
                            result[field] = add(result[field], add(mul(forward, after), mul(backward, before)))
                    after, before = neighbours(lambda *where: pair(axis_number, *where))
                    pressure, speed = acoustic(
                        axis_number, sound, after[0], before[0], after[1], before[1]
                    )
                    result[4] = add(result[4], pressure)
                    result[1 + axis_number] = add(result[1 + axis_number], speed)
                for field in range(5):
                    dst[field, dst_at + number, parity, line - dst_lines[0]] = result[field]
        return carry

    lax.fori_loop(0, count, layer, 0)


def gather_slots_kernel(others, at_ref, checkpoint, *rest):
    outs, sems = rest[:others], rest[others]
    copies = []
    for number in range(others):
        for slot in range(HELD_MOST):
            copies.append(
                pltpu.make_async_copy(
                    checkpoint.at[at_ref[number, slot]], outs[number].at[slot], sems.at[number, slot]
                )
            )
    for copy in copies:
        copy.start()
    for copy in copies:
        copy.wait()


def gather_slots(checkpoint, at):
    others = at.shape[0]
    piece = shape(HELD_MOST, *checkpoint.shape[1:])
    return pl.pallas_call(
        functools.partial(gather_slots_kernel, others),
        out_shape=[piece] * others,
        in_specs=[spec_smem(), spec_any()],
        out_specs=[spec_any()] * others,
        scratch_shapes=[pltpu.SemaphoreType.DMA((others, HELD_MOST))],
        compiler_params=params(),
        name="gather_slots",
    )(at, checkpoint)


def store_lines(lines, out, z):
    for line in range(4):
        rows = pl.ds(line * ROWS, ROWS)
        pressure = split_parity(lines[4, 0, rows, :], lines[4, 1, rows, :])
        for field in range(5):
            parts = pressure
            if field < 4:
                parts = split_parity(lines[field, 0, rows, :], lines[field, 1, rows, :])
            if field == 0:
                parts = (parts[0] - pressure[0], parts[1] - pressure[1])
            for parity in (0, 1):
                out[field, z, parity, line] = parts[parity]


def prepare_kernel(checkpoint, live, low, high, lines):
    slots = checkpoint.shape[0]
    for half, out in ((0, low), (1, high)):

        def held(z, carry, half=half, out=out):
            for field in range(5):
                for side in (0, 1):
                    for slot in range(slots):
                        lines[field, side, pl.ds(slot, 4, stride=ROWS), :] = checkpoint[
                            slot, field, half * DEPTH + z, :, pl.ds(side * LANES, LANES)
                        ]
            store_lines(lines, out.at[0], z)
            return carry

        def own(z, carry, half=half, out=out):
            for field in range(5):
                for side in (0, 1):
                    for group in range(4):
                        rows = live[field, half * DEPTH + z, pl.ds(group * ROWS, ROWS), pl.ds(side * LANES, LANES)]
                        for block in (0, 1):
                            lines[field, side, pl.ds(2 * group + block, 4, stride=ROWS), :] = rows[
                                4 * block : 4 * block + 4
                            ]
            store_lines(lines, out.at[1], z)
            return carry

        lax.fori_loop(0, DEPTH, held, 0)
        lax.fori_loop(0, DEPTH, own, 0)


def prepare(checkpoint, live):
    half = shape(2, 5, DEPTH, 2, 4, ROWS, LANES)
    return pl.pallas_call(
        prepare_kernel,
        out_shape=[half, half],
        in_specs=[spec_vmem(), spec_vmem()],
        out_specs=[spec_vmem(), spec_vmem()],
        scratch_shapes=[pltpu.VMEM((5, 2, 4 * ROWS, LANES), jnp.float32)],
        compiler_params=params(),
        name="prepare",
    )(checkpoint, live)


HELD_LINES = ((0, 4), (-1, 5), (-2, 6), (-3, 7), (-4, 8))
LIVE_LINES = ((0, 4),) * 5
CARRIES = ((0, 6), (0, 8), (0, 10), (1, 4), (1, 4), (1, 4))


def copy_all(pairs, sems):
    copies = [pltpu.make_async_copy(src, dst, sems.at[number]) for number, (src, dst) in enumerate(pairs)]
    for copy in copies:
        copy.start()
    for copy in copies:
        copy.wait()


def weigh_and_pack(others, held_out, live_out, rows_ref, mask_ref, tiles_ref, send, keep):
    def layer(z, carry):
        for field in (4, 0, 1, 2, 3):
            for parity in (0, 1):
                total = [live_out[field, z, parity, line] for line in range(4)]
                for other in range(others):
                    for place, first in ((0, 4), (1, 8), (2, 0)):
                        at = rows_ref[other, place]
                        mask = mask_ref[other, place]
                        for line in range(4):
                            image = held_out[field, z, parity, first + line]
                            total[line] = total[line] + mask * pick_rows(image, at)
                for number, out in ((0, send), (1, keep)):
                    at = tiles_ref[number, 0]
                    lower = tiles_ref[number, 1] == 0
                    for line in (0, 1):
                        value = jnp.where(lower, pick_rows(total[line], at), pick_rows(total[2 + line], at))
                        if field == 0:
                            value = value + out[4, z, parity, line]
                        out[field, z, parity, line] = value
        return carry

    lax.fori_loop(0, DEPTH, layer, 0)


def first_half_kernel(
    others, live_factors, held_factors, rows_ref, mask_ref, tiles_ref, before, low, high, *rest
):
    send, keep, *carries = rest[:8]
    held, live, h1, h2, h3, h4, l1, l2, l3, l4, sems = rest[8:]
    pairs = []
    for kind, state in ((0, held), (1, live)):
        for number, part in enumerate((before, low, high)):
            pairs.append((part.at[kind], state.at[:, pl.ds(number * DEPTH, DEPTH)]))
    copy_all(pairs, sems)
    run_sections(held, (h1, h2, h3, h4), HELD_LINES, False, held_factors, False)
    run_sections(live, (l1, l2, l3, l4), LIVE_LINES, True, live_factors, False)
    last = ((h1, 8), (h2, 6), (h3, 4), (l1, 8), (l2, 6), (l3, 4))
    copies = [
        pltpu.make_async_copy(src.at[:, pl.ds(at, 2)], out, sems.at[number])
        for number, ((src, at), out) in enumerate(zip(last, carries))
    ]
    for copy in copies:
        copy.start()
    weigh_and_pack(others, h4, l4, rows_ref, mask_ref, tiles_ref, send, keep)
    for copy in copies:
        copy.wait()


def second_half_kernel(
    others, live_factors, held_factors, rows_ref, mask_ref, tiles_ref, high, after, *rest
):
    carries, (send, keep) = rest[:6], rest[6:8]
    held, live, h1, h2, h3, h4, l1, l2, l3, l4, sems = rest[8:]
    pairs = []
    for kind, state in ((0, held), (1, live)):
        for number, part in enumerate((high, after)):
            pairs.append((part.at[kind], state.at[:, pl.ds(number * DEPTH, DEPTH)]))
    for carry, dst in zip(carries, (h1, h2, h3, l1, l2, l3)):
        pairs.append((carry, dst.at[:, pl.ds(0, 2)]))
    copy_all(pairs, sems)
    run_sections(held, (h1, h2, h3, h4), HELD_LINES, False, held_factors, True)
    run_sections(live, (l1, l2, l3, l4), LIVE_LINES, True, live_factors, True)
    weigh_and_pack(others, h4, l4, rows_ref, mask_ref, tiles_ref, send, keep)


def run_sections(state, stages, lines, wrap, factors, continued):
    for number in range(4):
        if wrap:
            row = [factors[number, i] for i in range(17)]
        else:
            row = [factors[number, i] for i in range(17)]
        src = state if number == 0 else stages[number - 1]
        if continued:
            src_at = 3 if number == 0 else 1
            state_at = 3 - number
            dst_at, count = (0 if number == 3 else 2), DEPTH
        else:
            src_at, state_at, dst_at, count = 1, 1 + number, 0, 3 * DEPTH - 2 * (number + 1)
        section(
            src, lines[number], src_at, state, state_at, stages[number], lines[number + 1], dst_at,
            count, row, wrap, number == 3,
        )


def half_step(kernel, parts, carries_in, tables, others, layers, last):
    live_factors, held_factors, rows, masks, tiles = tables
    packed = shape(5, DEPTH, 2, 2, ROWS, LANES)
    buffer = lambda count, lines: pltpu.VMEM((5, count, 2, lines, ROWS, LANES), jnp.float32)
    carry_shapes = [shape(5, 2, 2, lines, ROWS, LANES) for lines in (6, 8, 10, 4, 4, 4)]
    outs = [packed, packed] + ([] if last else carry_shapes)
    stage_layers = (6, 6, 6, DEPTH) if last else (10, 8, 6, DEPTH)
    return pl.pallas_call(
        functools.partial(kernel, others),
        out_shape=outs,
        in_specs=[spec_smem()] + [spec_vmem()] * 4 + [spec_any()] * (len(parts) + len(carries_in)),
        out_specs=[spec_vmem()] * 2 + [spec_any()] * (len(outs) - 2),
        scratch_shapes=[buffer(layers, 4), buffer(layers, 4)]
        + [buffer(count, lines) for count, lines in zip(stage_layers, (6, 8, 10, 12))]
        + [buffer(count, 4) for count in stage_layers]
        + [pltpu.SemaphoreType.DMA((10,))],
        compiler_params=params(),
        name="second_half" if last else "first_half",
    )(live_factors, held_factors, rows, masks, tiles, *parts, *carries_in)


def share_kernel(groups, at_ref, keep, arrived, *outs):
    def layer(z, carry):
        odd = lax.broadcasted_iota(jnp.int32, (ROWS, LANES), 0) % 2 == 1
        for field in range(5):
            for parity in (0, 1):
                first = keep[field, z, parity, 0] + arrived[field, z, parity, 0]
                second = keep[field, z, parity, 1] + arrived[field, z, parity, 1]
                for number in range(groups):
                    at = at_ref[number]
                    outs[number][field, z, parity] = jnp.where(
                        odd, pick_rows(second, at), pick_rows(first, at)
                    )
        return carry

    lax.fori_loop(0, DEPTH, layer, 0)


def share(keep, arrived, at):
    groups = at.shape[0]
    piece = shape(5, DEPTH, 2, ROWS, LANES)
    return pl.pallas_call(
        functools.partial(share_kernel, groups),
        out_shape=[piece] * groups,
        in_specs=[spec_vmem()] * 3,
        out_specs=[spec_vmem()] * groups,
        compiler_params=params(),
        name="share",
    )(at, keep, arrived)


def collect_kernel(groups, tile_most, swap_ref, mask_ref, *rest):
    pieces, out = rest[: 2 * groups], rest[2 * groups]
    swap = swap_ref[0] == 1
    for half in (0, 1):
        own = pieces[half * groups : (half + 1) * groups]

        def layer(z, carry, half=half, own=own):
            for field in range(5):
                sums = []
                for kind in (0, 1):
                    parts = []
                    for parity in (0, 1):
                        value = own[kind][field, z, parity]
                        for other in range(2 + kind, groups, 2):
                            value = value + own[other][field, z, parity]
                        parts.append(value)
                    sums.append(parts)
                for kind in (0, 1):
                    mask = mask_ref[kind]
                    parts = [
                        mask * jnp.where(swap, sums[1 - kind][parity], sums[kind][parity])
                        for parity in (0, 1)
                    ]
                    sides = join_parity(*parts)
                    for slot in range(tile_most // 2):
                        for side in (0, 1):
                            out[2 * slot + kind, field, half * DEPTH + z, :, pl.ds(side * LANES, LANES)] = sides[
                                side
                            ][2 * slot : 2 * slot + 2]
            return carry

        lax.fori_loop(0, DEPTH, layer, 0)


def collect(pieces, swap, masks, tile_most):
    groups = len(pieces) // 2
    return pl.pallas_call(
        functools.partial(collect_kernel, groups, tile_most),
        out_shape=shape(tile_most, 5, 2 * DEPTH, TILE_LINES, 2 * LANES),
        in_specs=[spec_smem()] + [spec_vmem()] * (1 + len(pieces)),
        out_specs=spec_vmem(),
        compiler_params=params(),
        name="collect",
    )(swap, masks, *pieces)


def place_kernel(others, block_ref, *rest):
    pieces, (low, high, lines) = rest[:others], rest[others:]
    for half, out in ((0, low), (1, high)):

        def layer(z, carry, half=half, out=out):
            for number in range(others):
                for slot in range(HELD_MOST):
                    block = block_ref[number, slot]

                    @pl.when(block >= 0)
                    def _():
                        for field in range(5):
                            for side in (0, 1):
                                lines[field, side, pl.ds(block, 4, stride=ROWS), :] = pieces[number][
                                    slot, field, half * DEPTH + z, :, pl.ds(side * LANES, LANES)
                                ]

            store_lines(lines, out, z)
            return carry

        lax.fori_loop(0, DEPTH, layer, 0)


def place(pieces, blocks):
    half = shape(5, DEPTH, 2, 4, ROWS, LANES)
    return pl.pallas_call(
        functools.partial(place_kernel, len(pieces)),
        out_shape=[half, half],
        in_specs=[spec_smem()] + [spec_vmem()] * len(pieces),
        out_specs=[spec_vmem()] * 2,
        scratch_shapes=[pltpu.VMEM((5, 2, 4 * ROWS, LANES), jnp.float32)],
        compiler_params=params(),
        name="place",
    )(blocks, *pieces)


def recover_kernel(factors, before, low, high, after, out, state, s1, s2, s3, s4, lines, sems):
    copy_all(
        [(part, state.at[:, pl.ds(number * DEPTH, DEPTH)]) for number, part in enumerate((before, low, high, after))],
        sems,
    )
    for number, dst in enumerate((s1, s2, s3, s4)):
        src = state if number == 0 else (s1, s2, s3)[number - 1]
        row = [factors[number, i] for i in range(17)]
        section(src, (0, 4), 1, state, 1 + number, dst, (0, 4), 0, 4 * DEPTH - 2 * (number + 1), row, True, False)

    def layer(z, carry):
        for line in range(4):
            pressure = [s4[4, z, parity, line] for parity in (0, 1)]
            for field in range(5):
                parts = pressure if field == 4 else [s4[field, z, parity, line] for parity in (0, 1)]
                if field == 0:
                    parts = [parts[parity] + pressure[parity] for parity in (0, 1)]
                for side, value in enumerate(join_parity(*parts)):
                    lines[field, side, pl.ds(line, ROWS, stride=4), :] = value
        for field in range(5):
            for side in (0, 1):
                out[field, z, :, pl.ds(side * LANES, LANES)] = lines[field, side]
        return carry

    lax.fori_loop(0, 2 * DEPTH, layer, 0)


def recover(factors, parts):
    buffer = lambda count: pltpu.VMEM((5, count, 2, 4, ROWS, LANES), jnp.float32)
    return pl.pallas_call(
        recover_kernel,
        out_shape=shape(5, 2 * DEPTH, 4 * ROWS, 2 * LANES),
        in_specs=[spec_smem()] + [spec_any()] * 4,
        out_specs=spec_vmem(),
        scratch_shapes=[buffer(count) for count in (16, 14, 12, 10, 8)]
        + [pltpu.VMEM((5, 2, 4 * ROWS, LANES), jnp.float32), pltpu.SemaphoreType.DMA((4,))],
        compiler_params=params(),
        name="recover",
    )(factors, *parts)


def rows_of(table):
    return jnp.broadcast_to(table[..., None], (*table.shape, LANES))


def body(checkpoint, slot_block, live_state, levels, coefficients, tile_owner):
    groups = lax.axis_size("buddy")
    slabs = lax.axis_size("slab")
    myself = lax.axis_index("buddy")
    others = groups - 1
    blocks = checkpoint.shape[0]
    partners = [jnp.bitwise_xor(myself, d) for d in range(groups)]
    distances = jnp.arange(1, groups, dtype=jnp.int32)
    other_grids = jnp.bitwise_xor(myself, distances)
    trade = lambda array, d: lax.ppermute(array, "buddy", [(i, i ^ d) for i in range(groups)])
    upward = lambda array: lax.ppermute(array, "slab", [(i, (i + 1) % slabs) for i in range(slabs)])
    downward = lambda array: lax.ppermute(array, "slab", [((i + 1) % slabs, i) for i in range(slabs)])

    slot_grid, slot_place = slot_block // blocks, slot_block % blocks
    earlier = jnp.tril(jnp.ones((blocks, blocks), jnp.int32), -1)
    same = (slot_grid[:, :, None] == slot_grid[:, None, :]).astype(jnp.int32)
    slot_rank = jnp.sum(same * earlier[None], axis=2)
    held_grid = lax.dynamic_index_in_dim(slot_grid, myself, 0, keepdims=False)
    held_place = lax.dynamic_index_in_dim(slot_place, myself, 0, keepdims=False)
    held_rank = lax.dynamic_index_in_dim(slot_rank, myself, 0, keepdims=False)
    slots = jnp.arange(blocks, dtype=jnp.int32)
    wanted = (held_grid[None, None, :] == other_grids[:, None, None]) & (
        held_rank[None, None, :] == jnp.arange(HELD_MOST, dtype=jnp.int32)[None, :, None]
    )
    send_at = jnp.sum(jnp.where(wanted, slots, 0), axis=2).astype(jnp.int32)
    sent = gather_slots(checkpoint, send_at)
    received = [trade(array, d) for d, array in enumerate(sent, 1)]

    low, high = prepare(checkpoint, live_state[0])
    before = upward(high)
    after = downward(low)

    inverse = jnp.exp2(levels[:, 0, :].astype(jnp.float32))
    facts = lax.all_gather(jnp.concatenate([inverse[0], coefficients[0]]), "buddy", axis=0)
    waves = [abs(drift) + 1.0 for drift in VELOCITY]

    def factors_of(spacing, weight):
        spread = waves[0] * spacing[0] + waves[1] * spacing[1] + waves[2] * spacing[2]
        return factor_table(spacing, COURANT / spread, weight)

    recover_factors = factors_of([inverse[0, a] for a in range(3)], jnp.float32(1.0))
    live_factors = factors_of([inverse[1, a] for a in range(3)], coefficients[1, 0])
    of_slot = (held_grid[:, None] == jnp.arange(groups, dtype=jnp.int32)[None, :])
    slot_facts = jnp.sum(jnp.where(of_slot[:, :, None], facts[None], 0.0), axis=1)
    held_factors = rows_of(factors_of([slot_facts[:, a] for a in range(3)], slot_facts[:, 3]))

    rows, masks = [], []
    for shift in (0, 1, -1):
        place_wanted = (slots - shift) % blocks
        hit = (held_grid[None, None, :] == other_grids[:, None, None]) & (
            held_place[None, None, :] == place_wanted[None, :, None]
        )
        rows.append(jnp.sum(jnp.where(hit, slots, 0), axis=2).astype(jnp.int32))
        masks.append(jnp.sum(hit.astype(jnp.float32), axis=2))
    rows = rows_of(jnp.stack(rows, 1))
    masks = rows_of(jnp.stack(masks, 1))

    own_tiles = tile_owner[0]
    tile_count = own_tiles.shape[0]
    tile_most = 2 * tile_count // groups
    numbers = jnp.arange(tile_count, dtype=jnp.int32)
    ahead = (own_tiles[None, :] < own_tiles[:, None]) | (
        (own_tiles[None, :] == own_tiles[:, None]) & (numbers[None, :] < numbers[:, None])
    )
    position = jnp.sum(ahead.astype(jnp.int32), axis=1)
    readers = jnp.arange(groups, dtype=jnp.int32)
    start = jnp.sum((own_tiles[None, :] < readers[:, None]).astype(jnp.int32), axis=1)
    amount = jnp.sum((own_tiles[None, :] == readers[:, None]).astype(jnp.int32), axis=1)
    kind = myself % 2
    order = jnp.stack([2 * slots + 1 - kind, 2 * slots + kind])
    listed = jnp.sum(jnp.where(position[None, None, :] == order[:, :, None], numbers, 0), axis=2)
    tiles = rows_of(jnp.stack([listed // 2, listed % 2], 1).astype(jnp.int32))
    first_slot = (start + 1 - kind) // 2
    partner_first = jnp.sum(
        jnp.where(jnp.stack(partners)[:, None] == readers[None, :], first_slot[None, :], 0), axis=1
    )
    share_at = rows_of(jnp.minimum(partner_first[:, None] + slots[None, :] // 2, ROWS - 1))
    my_start = jnp.sum(jnp.where(readers == myself, start, 0))
    my_amount = jnp.sum(jnp.where(readers == myself, amount, 0))
    swap = ((my_start % 2) != kind).astype(jnp.int32).reshape(1)
    tile_ranks = 2 * (slots[None, :] // 2) + jnp.arange(2, dtype=jnp.int32)[:, None]
    tile_masks = rows_of((tile_ranks < my_amount).astype(jnp.float32))

    tables = (live_factors, held_factors, rows, masks, tiles)
    send_low, keep_low, *carries = half_step(
        first_half_kernel, (before, low, high), (), tables, others, 3 * DEPTH, False
    )
    arrived_low = trade(send_low, 1)
    send_high, keep_high = half_step(
        second_half_kernel, (high, after), carries, tables, others, 2 * DEPTH, True
    )
    arrived_high = trade(send_high, 1)

    shares_low = share(keep_low, arrived_low, share_at)
    pieces_low = [shares_low[0]] + [trade(shares_low[d], d) for d in range(1, groups)]
    shares_high = share(keep_high, arrived_high, share_at)
    pieces_high = [shares_high[0]] + [trade(shares_high[d], d) for d in range(1, groups)]

    received_blocks = []
    for d in range(1, groups):
        holder_grid = lax.dynamic_index_in_dim(slot_grid, partners[d], 0, keepdims=False)
        holder_place = lax.dynamic_index_in_dim(slot_place, partners[d], 0, keepdims=False)
        holder_rank = lax.dynamic_index_in_dim(slot_rank, partners[d], 0, keepdims=False)
        hit = (holder_grid[None, :] == myself) & (
            holder_rank[None, :] == jnp.arange(HELD_MOST, dtype=jnp.int32)[:, None]
        )
        received_blocks.append(jnp.sum(jnp.where(hit, holder_place[None, :] + 1, 0), axis=1) - 1)
    restored_low, restored_high = place(received, jnp.stack(received_blocks).astype(jnp.int32))
    restored_before = upward(restored_high)
    restored_after = downward(restored_low)
    recovered = recover(recover_factors, (restored_before, restored_low, restored_high, restored_after))
    combined = collect(pieces_low + pieces_high, swap, tile_masks, tile_most)
    return recovered[None], combined


def solution(mesh):
    return jax.shard_map(
        body,
        mesh=mesh,
        in_specs=(
            P("buddy", None, "slab", None, None),
            P(),
            P("buddy", None, "slab", None, None),
            P(None, "buddy", None),
            P(None, "buddy"),
            P("slab", None),
        ),
        out_specs=(P("buddy", None, "slab", None, None), P("buddy", None, "slab", None, None)),
        check_vma=False,
    )
```

```python
import functools

import jax
import jax.numpy as jnp
from jax import lax
from jax.experimental import pallas as pl
from jax.experimental.pallas import tpu as pltpu
from jax.sharding import PartitionSpec as P

VELOCITY = (0.3, -0.2, 0.45)
COURANT = 1.0
TILE_LINES = 2
HELD_MOST = 3
DEPTH = 4
LANES = 128
ROWS = 8
VMEM_BYTES = 32 * 1024 * 1024


def spec_vmem():
    return pl.BlockSpec(memory_space=pltpu.VMEM)


def spec_smem():
    return pl.BlockSpec(memory_space=pltpu.SMEM)


def spec_any():
    return pl.BlockSpec(memory_space=pl.ANY)


def spec_hbm():
    return pl.BlockSpec(memory_space=pltpu.HBM)


def params():
    return pltpu.CompilerParams(vmem_limit_bytes=VMEM_BYTES)


def cost(microseconds, flops=0):
    return pl.CostEstimate(flops=flops, bytes_accessed=microseconds, transcendentals=0)


def shape(*dims):
    return jax.ShapeDtypeStruct(dims, jnp.float32)


def add(*terms):
    total = None
    for term in terms:
        if term is not None:
            total = term if total is None else total + term
    return total


def sub(left, right):
    if right is None:
        return left
    return -right if left is None else left - right


def mul(factor, term):
    return None if term is None else factor * term


def lane_index():
    return lax.broadcasted_iota(jnp.int32, (ROWS, LANES), 1)


def turn_lanes(value, amount):
    return None if value is None else pltpu.roll(value, amount, 1)


def one_hot(out, join):
    row = lax.broadcasted_iota(jnp.int32, (LANES, 2 * LANES), 0)
    column = lax.broadcasted_iota(jnp.int32, (LANES, 2 * LANES), 1)
    for part in (0, 1):
        if join:
            target = 2 * row + part
        else:
            cell = row + part * LANES
            target = cell // 2 + LANES * (cell % 2)
        out[part] = (column == target).astype(jnp.float32).astype(jnp.bfloat16)


def move_lanes(rows, matrix):
    top = rows.astype(jnp.bfloat16)
    rest = rows - top.astype(jnp.float32)
    middle = rest.astype(jnp.bfloat16)
    low = (rest - middle.astype(jnp.float32)).astype(jnp.bfloat16)
    product = lambda part: jnp.dot(part, matrix, preferred_element_type=jnp.float32)
    return (product(top) + product(middle)) + product(low)


def one_hot_scratch():
    return pltpu.VMEM((2, LANES, 2 * LANES), jnp.bfloat16)


def pick_rows(array, at):
    return jnp.take_along_axis(array, at, axis=0)


def direction_factors(axis_number):
    drift = VELOCITY[axis_number]
    wave = abs(drift) + 1.0
    carried = (0.5 * (wave - drift), 0.5 * (wave + drift))
    if drift >= 0:
        rising = (0.0, 0.5 * wave)
        falling = (0.5, 0.5 * drift)
    else:
        rising = (-0.5 * drift, 0.5)
        falling = (0.5 * wave, 0.0)
    return carried, rising, falling


def store_factors(out, spacing, weight):
    waves = [abs(drift) + 1.0 for drift in VELOCITY]
    spread = (waves[0] * spacing[0] + waves[1] * spacing[1]) + waves[2] * spacing[2]
    time_step = COURANT / spread
    for number, part in enumerate((4.0, 3.0, 2.0, 1.0)):
        scale = time_step * (1.0 / part)
        if number == 3:
            scale = scale * weight
        out[number, 0] = -(scale * spread)
        for axis_number in range(3):
            unit = scale * spacing[axis_number]
            carried, rising, falling = direction_factors(axis_number)
            one_sided = rising if 0.0 in rising else falling
            two_sided = falling if 0.0 in rising else rising
            for place, factor in enumerate((*carried, one_sided[0] + one_sided[1], *two_sided)):
                out[number, 1 + 5 * axis_number + place] = unit * factor
        out[number, 16] = weight


def splat(scalar):
    return jnp.full((ROWS, LANES), scalar, jnp.float32)


def spacing_of(level):
    return lax.shift_left(jnp.int32(1), level).astype(jnp.float32)


def own_factors(out, levels_ref, kind, weight):
    store_factors(out, [splat(spacing_of(levels_ref[kind, 0, axis])) for axis in range(3)], splat(weight))


def row_index():
    return lax.broadcasted_iota(jnp.int32, (ROWS, LANES), 0)


def by_slot(scalars):
    value = splat(scalars[0])
    for slot, scalar in enumerate(scalars[1:], 1):
        value = jnp.where(row_index() == slot, scalar, value)
    return value


def held_tables(me, block_ref, fact_refs, facts, factors, rows, masks):
    slots = block_ref.shape[1]
    for number, ref in enumerate(fact_refs):
        for item in range(3):
            facts[number, item] = spacing_of(ref[item].astype(jnp.int32))
        facts[number, 3] = ref[6]
    grids = [block_ref[me, slot] // slots for slot in range(slots)]
    places = [block_ref[me, slot] % slots for slot in range(slots)]
    numbers = [jnp.bitwise_xor(grid, me) - 1 for grid in grids]
    columns = [by_slot([facts[number, item] for number in numbers]) for item in range(4)]
    store_factors(factors, columns[:3], columns[3])
    for other in range(len(fact_refs)):
        for place, shift in enumerate((0, 1, -1)):
            at = jnp.zeros((ROWS, LANES), jnp.int32)
            mask = jnp.zeros((ROWS, LANES), jnp.float32)
            for slot in range(slots):
                target = jnp.where(numbers[slot] == other, (places[slot] + shift) % slots, -1)
                hit = row_index() == target
                at = jnp.where(hit, slot, at)
                mask = jnp.where(hit, 1.0, mask)
            rows[other, place] = at
            masks[other, place] = mask


def count_tiles(owner_ref, groups, start, amount, rank):
    for reader in range(groups):
        amount[reader] = 0
    for tile in range(owner_ref.shape[1]):
        reader = owner_ref[0, tile]
        rank[tile] = amount[reader]
        amount[reader] = amount[reader] + 1
    total = jnp.int32(0)
    for reader in range(groups):
        start[reader] = total
        total = total + amount[reader]


def tile_scratch(groups, tiles):
    return [pltpu.SMEM((groups,), jnp.int32), pltpu.SMEM((groups,), jnp.int32), pltpu.SMEM((tiles,), jnp.int32)]


def first_slot(start, kind):
    return (start + 1 - kind) // 2


def tile_tables(me, owner_ref, groups, counts, table):
    start, amount, rank = counts
    count_tiles(owner_ref, groups, start, amount, rank)
    kind = me % 2
    lists = [[jnp.zeros((ROWS, LANES), jnp.int32) for _ in range(2)] for _ in range(2)]
    for tile in range(owner_ref.shape[1]):
        position = start[owner_ref[0, tile]] + rank[tile]
        for number in (0, 1):
            mine = position % 2 == (kind if number == 1 else 1 - kind)
            hit = row_index() == jnp.where(mine, position // 2, -1)
            lists[number][0] = jnp.where(hit, tile // 2, lists[number][0])
            lists[number][1] = jnp.where(hit, tile % 2, lists[number][1])
    for number in (0, 1):
        for item in (0, 1):
            table[number, item] = lists[number][item]


def acoustic(axis_number, factors, rising_next, rising_prev, falling_next, falling_prev):
    one, two_next, two_prev = factors
    if VELOCITY[axis_number] >= 0:
        rising = mul(one, rising_prev)
        falling = add(mul(two_next, falling_next), mul(two_prev, falling_prev))
    else:
        rising = add(mul(two_next, rising_next), mul(two_prev, rising_prev))
        falling = mul(one, falling_next)
    return add(rising, falling), sub(rising, falling)


def section(src, src_lines, src_at, state, state_at, dst, dst_lines, dst_at, count, factors, wrap, scaled):
    def layer(number, carry):
        cache = {}

        def cell(field, parity, line, step=0):
            low, high = src_lines
            key = (field, parity, line, step)
            if key in cache:
                return cache[key]
            if low <= line < high:
                value = src[field, src_at + number + step, parity, line - low]
            elif wrap and line < low:
                value = pltpu.roll(cell(field, parity, high - 1), 1, 0)
            elif wrap:
                value = pltpu.roll(cell(field, parity, low), ROWS - 1, 0)
            else:
                value = None
            cache[key] = value
            return value

        def pair(axis_number, parity, line, step=0):
            key = ("pair", axis_number, parity, line, step)
            if key not in cache:
                pressure = cell(4, parity, line, step)
                speed = cell(1 + axis_number, parity, line, step)
                cache[key] = (None, None) if pressure is None else (pressure + speed, pressure - speed)
            return cache[key]

        centre = factors[0]
        for line in range(*dst_lines):
            for parity in (0, 1):
                result = [None] * 5
                for field in range(5):
                    terms = mul(centre, cell(field, parity, line))
                    if 0 <= line < 4:
                        held = state[field, state_at + number, parity, line]
                        terms = add(mul(factors[16], held) if scaled else held, terms)
                    result[field] = terms
                for axis_number in range(3):
                    forward, backward, *sound = factors[1 + 5 * axis_number : 6 + 5 * axis_number]

                    def neighbours(read):
                        if axis_number == 0:
                            other = read(1 - parity, line, 0)
                            if parity == 0:
                                return other, [turn_lanes(part, 1) for part in other]
                            return [turn_lanes(part, LANES - 1) for part in other], other
                        if axis_number == 1:
                            return read(parity, line + 1, 0), read(parity, line - 1, 0)
                        return read(parity, line, 1), read(parity, line, -1)

                    for field in range(4):
                        if field != 1 + axis_number:
                            (after,), (before,) = neighbours(
                                lambda *where, field=field: [cell(field, *where)]
                            )
                            result[field] = add(result[field], add(mul(forward, after), mul(backward, before)))
                    after, before = neighbours(lambda *where: pair(axis_number, *where))
                    pressure, speed = acoustic(
                        axis_number, sound, after[0], before[0], after[1], before[1]
                    )
                    result[4] = add(result[4], pressure)
                    result[1 + axis_number] = add(result[1 + axis_number], speed)
                for field in range(5):
                    dst[field, dst_at + number, parity, line - dst_lines[0]] = result[field]
        return carry

    lax.fori_loop(0, count, layer, 0)


def gather_slots_kernel(others, me_ref, block_ref, checkpoint, *outs):
    me = me_ref[0]
    slots = checkpoint.shape[0]
    grids = [block_ref[me, slot] // slots for slot in range(slots)]
    for slot in range(slots):
        rank = jnp.int32(0)
        for earlier in range(slot):
            rank = rank + (grids[earlier] == grids[slot]).astype(jnp.int32)
        for number in range(others):

            @pl.when(grids[slot] == jnp.bitwise_xor(me, number + 1))
            def _(slot=slot, number=number, rank=rank):
                def layer(z, carry):
                    for field in range(5):
                        outs[number][rank, field, z] = checkpoint[slot, field, z]
                    return carry

                lax.fori_loop(0, checkpoint.shape[2], layer, 0)


def gather_slots(me, slot_block, checkpoint, others):
    piece = shape(HELD_MOST, *checkpoint.shape[1:])
    return pl.pallas_call(
        functools.partial(gather_slots_kernel, others),
        out_shape=[piece] * others,
        in_specs=[spec_smem(), spec_smem(), spec_vmem()],
        out_specs=[spec_vmem()] * others,
        compiler_params=params(),
        cost_estimate=cost(1),
        name="gather_slots",
    )(me, slot_block, checkpoint)


def store_lines(lines, matrix, out, z):
    halves = [lines[:, side].reshape(5 * 4 * ROWS, LANES) for side in (0, 1)]
    moved = move_lanes(halves[0], matrix[0]) + move_lanes(halves[1], matrix[1])
    moved = moved.reshape(5, 4, ROWS, 2 * LANES)
    for parity in (0, 1):
        lanes = slice(parity * LANES, (parity + 1) * LANES)
        out[0, z, parity] = moved[0, :, :, lanes] - moved[4, :, :, lanes]
        for field in range(1, 5):
            out[field, z, parity] = moved[field, :, :, lanes]


def prepare_kernel(checkpoint, live, low, high, held_lines, own_lines, matrix):
    slots = checkpoint.shape[0]
    one_hot(matrix, False)

    for half, out in ((1, high), (0, low)):

        def layer(z, carry, half=half, out=out):
            for field in range(5):
                for side in (0, 1):
                    lanes = pl.ds(side * LANES, LANES)
                    for slot in range(slots):
                        held_lines[field, side, pl.ds(slot, 4, stride=ROWS), :] = checkpoint[
                            slot, field, half * DEPTH + z, :, lanes
                        ]
                    for group in range(4):
                        rows = live[field, half * DEPTH + z, pl.ds(group * ROWS, ROWS), lanes]
                        for block in (0, 1):
                            own_lines[field, side, pl.ds(2 * group + block, 4, stride=ROWS), :] = rows[
                                4 * block : 4 * block + 4
                            ]
            store_lines(held_lines, matrix, out.at[0], z)
            store_lines(own_lines, matrix, out.at[1], z)
            return carry

        lax.fori_loop(0, DEPTH, layer, 0)


def prepare(checkpoint, live):
    lines = pltpu.VMEM((5, 2, 4 * ROWS, LANES), jnp.float32)
    half = shape(2, 5, DEPTH, 2, 4, ROWS, LANES)
    return pl.pallas_call(
        prepare_kernel,
        out_shape=[half, half],
        in_specs=[spec_vmem(), spec_vmem()],
        out_specs=[spec_vmem(), spec_vmem()],
        scratch_shapes=[lines, lines, one_hot_scratch()],
        compiler_params=params(),
        cost_estimate=cost(1),
        name="prepare",
    )(checkpoint, live)


HELD_LINES = ((0, 4), (-1, 5), (-2, 6), (-3, 7), (-4, 8))
LIVE_LINES = ((0, 4),) * 5
CARRIES = ((0, 6), (0, 8), (0, 10), (1, 4), (1, 4), (1, 4))


def copy_layers(src, src_at, dst, dst_at, count):
    def layer(z, carry):
        dst[:, dst_at + z] = src[:, src_at + z]
        return carry

    lax.fori_loop(0, count, layer, 0)


def weigh_and_pack(others, held_out, live_out, rows_ref, mask_ref, tiles_ref, send, keep):
    def layer(z, carry):
        for field in (4, 0, 1, 2, 3):
            for parity in (0, 1):
                total = [live_out[field, z, parity, line] for line in range(4)]
                for other in range(others):
                    for place, first in ((0, 4), (1, 8), (2, 0)):
                        at = rows_ref[other, place]
                        mask = mask_ref[other, place]
                        for line in range(4):
                            image = held_out[field, z, parity, first + line]
                            total[line] = total[line] + mask * pick_rows(image, at)
                for number, out in ((0, send), (1, keep)):
                    at = tiles_ref[number, 0]
                    lower = tiles_ref[number, 1] == 0
                    for line in (0, 1):
                        value = jnp.where(lower, pick_rows(total[line], at), pick_rows(total[2 + line], at))
                        if field == 0:
                            value = value + out[4, z, parity, line]
                        out[field, z, parity, line] = value
        return carry

    lax.fori_loop(0, DEPTH, layer, 0)


def half_tables(others, scalars, scratch):
    me_ref, block_ref, owner_ref, levels_ref, weights_ref, *fact_refs = scalars
    live_factors, held_factors, rows, masks, tiles, facts, *counts = scratch
    me = me_ref[0]
    own_factors(live_factors, levels_ref, 1, weights_ref[1, 0])
    held_tables(me, block_ref, fact_refs, facts, held_factors, rows, masks)
    tile_tables(me, owner_ref, others + 1, counts, tiles)
    return live_factors, held_factors, rows, masks, tiles


def start_halo(part, held, live, at, sems):
    copies = [
        pltpu.make_async_copy(part.at[kind], state.at[:, pl.ds(at, DEPTH)], sems.at[kind])
        for kind, state in ((0, held), (1, live))
    ]
    for copy in copies:
        copy.start()
    return copies


def first_half_kernel(others, *refs):
    scalars, refs = refs[: 5 + others], refs[5 + others :]
    before, low, high, send, keep, *refs = refs
    carries, refs = refs[:6], refs[6:]
    held, live, h1, h2, h3, h4, l1, l2, l3, l4, sems, *scratch = refs
    waiting = start_halo(before, held, live, 0, sems)
    for kind, state in ((0, held), (1, live)):
        for number, part in ((1, low), (2, high)):
            copy_layers(part.at[kind], 0, state, number * DEPTH, DEPTH)
    live_factors, held_factors, rows, masks, tiles = half_tables(others, scalars, scratch)
    waiting[0].wait()
    run_sections(held, (h1, h2, h3, h4), HELD_LINES, False, held_factors, False)
    waiting[1].wait()
    run_sections(live, (l1, l2, l3, l4), LIVE_LINES, True, live_factors, False)
    last = ((h1, 8), (h2, 6), (h3, 4), (l1, 8), (l2, 6), (l3, 4))
    for (src, at), out in zip(last, carries):
        copy_layers(src, at, out, 0, 2)
    weigh_and_pack(others, h4, l4, rows, masks, tiles, send, keep)


def second_half_kernel(others, *refs):
    scalars, refs = refs[: 5 + others], refs[5 + others :]
    after, high, *refs = refs
    carries, (send, keep, *refs) = refs[:6], refs[6:]
    held, live, h1, h2, h3, h4, l1, l2, l3, l4, sems, *scratch = refs
    waiting = start_halo(after, held, live, DEPTH, sems)
    for kind, state in ((0, held), (1, live)):
        copy_layers(high.at[kind], 0, state, 0, DEPTH)
    for carry, dst in zip(carries, (h1, h2, h3, l1, l2, l3)):
        copy_layers(carry, 0, dst, 0, 2)
    live_factors, held_factors, rows, masks, tiles = half_tables(others, scalars, scratch)
    waiting[0].wait()
    run_sections(held, (h1, h2, h3, h4), HELD_LINES, False, held_factors, True)
    waiting[1].wait()
    run_sections(live, (l1, l2, l3, l4), LIVE_LINES, True, live_factors, True)
    weigh_and_pack(others, h4, l4, rows, masks, tiles, send, keep)


def run_sections(state, stages, lines, wrap, factors, continued):
    for number in range(4):
        row = [factors[number, i] for i in range(17)]
        src = state if number == 0 else stages[number - 1]
        if continued:
            src_at = 3 if number == 0 else 1
            state_at = 3 - number
            dst_at, count = (0 if number == 3 else 2), DEPTH
        else:
            src_at, state_at, dst_at, count = 1, 1 + number, 0, 3 * DEPTH - 2 * (number + 1)
        section(
            src, lines[number], src_at, state, state_at, stages[number], lines[number + 1], dst_at,
            count, row, wrap, number == 3,
        )


def half_step(kernel, scalars, parts, carries_in, layers, last):
    others = len(scalars) - 5
    tiles = scalars[2].shape[1]
    packed = shape(5, DEPTH, 2, 2, ROWS, LANES)
    buffer = lambda count, lines: pltpu.VMEM((5, count, 2, lines, ROWS, LANES), jnp.float32)
    table = lambda *dims, kind=jnp.float32: pltpu.VMEM((*dims, ROWS, LANES), kind)
    carry_shapes = [shape(5, 2, 2, lines, ROWS, LANES) for lines in (6, 8, 10, 4, 4, 4)]
    outs = [packed, packed] + ([] if last else carry_shapes)
    stage_layers = (6, 6, 6, DEPTH) if last else (10, 8, 6, DEPTH)
    return pl.pallas_call(
        functools.partial(kernel, others),
        out_shape=outs,
        in_specs=[spec_smem()] * len(scalars) + [spec_any()] + [spec_vmem()] * (len(parts) - 1 + len(carries_in)),
        out_specs=[spec_vmem()] * len(outs),
        scratch_shapes=[buffer(layers, 4), buffer(layers, 4)]
        + [buffer(count, lines) for count, lines in zip(stage_layers, (6, 8, 10, 12))]
        + [buffer(count, 4) for count in stage_layers]
        + [pltpu.SemaphoreType.DMA((2,))]
        + [table(4, 17), table(4, 17), table(others, 3, kind=jnp.int32), table(others, 3), table(2, 2, kind=jnp.int32)]
        + [pltpu.SMEM((others, 4), jnp.float32)]
        + tile_scratch(others + 1, tiles),
        compiler_params=params(),
        cost_estimate=cost(8 if last else 12),
        name="second_half" if last else "first_half",
    )(*scalars, *parts, *carries_in)


def share_kernel(groups, me_ref, owner_ref, keep_low, arrived_low, keep_high, arrived_high, *refs):
    outs, (table, *counts) = refs[:groups], refs[groups:]
    start = counts[0]
    count_tiles(owner_ref, groups, *counts)
    me = me_ref[0]
    for number in range(groups):
        first = first_slot(start[jnp.bitwise_xor(me, number)], me % 2)
        table[number] = jnp.minimum(first + row_index() // 2, ROWS - 1)

    for half, keep, arrived in ((0, keep_low, arrived_low), (1, keep_high, arrived_high)):

        def layer(z, carry, half=half, keep=keep, arrived=arrived):
            odd = row_index() % 2 == 1
            for field in range(5):
                for parity in (0, 1):
                    first = keep[field, z, parity, 0] + arrived[field, z, parity, 0]
                    second = keep[field, z, parity, 1] + arrived[field, z, parity, 1]
                    for number in range(groups):
                        at = table[number]
                        outs[number][field, half * DEPTH + z, parity] = jnp.where(
                            odd, pick_rows(second, at), pick_rows(first, at)
                        )
            return carry

        lax.fori_loop(0, DEPTH, layer, 0)


def share(me, owner, halves, groups):
    piece = shape(5, 2 * DEPTH, 2, ROWS, LANES)
    return pl.pallas_call(
        functools.partial(share_kernel, groups),
        out_shape=[piece] * groups,
        in_specs=[spec_smem()] * 2 + [spec_vmem()] * len(halves),
        out_specs=[spec_vmem()] * groups,
        scratch_shapes=[pltpu.VMEM((groups, ROWS, LANES), jnp.int32)] + tile_scratch(groups, owner.shape[1]),
        compiler_params=params(),
        cost_estimate=cost(1),
        name="share",
    )(me, owner, *halves)


def collect_kernel(groups, tile_most, me_ref, owner_ref, *rest):
    pieces, (out, matrix, *counts) = rest[:groups], rest[groups:]
    count_tiles(owner_ref, groups, *counts)
    one_hot(matrix, True)
    me = me_ref[0]
    mine = counts[1][me]
    swap = counts[0][me] % 2 != me % 2

    def layer(z, carry):
        even = 2 * (row_index() // 2) < mine
        odd = 2 * (row_index() // 2) + 1 < mine
        moved = None
        for parity in (0, 1):
            sums = []
            for kind in (0, 1):
                value = pieces[kind][:, z, parity]
                for other in range(2 + kind, groups, 2):
                    value = value + pieces[other][:, z, parity]
                sums.append(value)
            rows = jnp.concatenate(
                [
                    jnp.where(even, jnp.where(swap, sums[1], sums[0]), 0.0),
                    jnp.where(odd, jnp.where(swap, sums[0], sums[1]), 0.0),
                ]
            )
            part = move_lanes(rows.reshape(10 * ROWS, LANES), matrix[parity])
            moved = part if moved is None else moved + part
        moved = moved.reshape(2, 5, ROWS, 2 * LANES)
        for kind in (0, 1):
            for field in range(5):
                for slot in range(tile_most // 2):
                    out[2 * slot + kind, field, z] = moved[kind, field, 2 * slot : 2 * slot + 2]
        return carry

    lax.fori_loop(0, 2 * DEPTH, layer, 0)


def collect(me, owner, pieces, tile_most):
    groups = len(pieces)
    return pl.pallas_call(
        functools.partial(collect_kernel, groups, tile_most),
        out_shape=shape(tile_most, 5, 2 * DEPTH, TILE_LINES, 2 * LANES),
        in_specs=[spec_smem()] * 2 + [spec_vmem()] * len(pieces),
        out_specs=spec_vmem(),
        scratch_shapes=[one_hot_scratch()] + tile_scratch(groups, owner.shape[1]),
        compiler_params=params(),
        cost_estimate=cost(2),
        name="collect",
    )(me, owner, *pieces)


def place_kernel(others, me_ref, block_ref, *rest):
    pieces, (low, high, lines, matrix, table) = rest[:others], rest[others:]
    one_hot(matrix, False)
    me = me_ref[0]
    slots = block_ref.shape[1]
    groups = block_ref.shape[0]
    inner = (me == groups // 2 - 1) | (me == groups // 2)
    for number in range(others):
        for slot in range(HELD_MOST):
            table[number, slot] = -1
        holder = jnp.bitwise_xor(me, min(number + 1, groups - 1))
        rank = jnp.int32(0)
        for slot in range(slots):
            block = block_ref[holder, slot]
            mine = block // slots == me
            if number >= groups - 2:
                mine = mine & (inner if number == groups - 1 else jnp.logical_not(inner))
            table[number, jnp.where(mine, rank, HELD_MOST)] = block % slots
            rank = rank + mine.astype(jnp.int32)
    for half, out in ((0, low), (1, high)):

        def layer(z, carry, half=half, out=out):
            for number in range(others):
                for slot in range(HELD_MOST):
                    block = table[number, slot]

                    @pl.when(block >= 0)
                    def _(number=number, slot=slot, block=block):
                        for field in range(5):
                            for side in (0, 1):
                                lines[field, side, pl.ds(block, 4, stride=ROWS), :] = pieces[number][
                                    slot, field, half * DEPTH + z, :, pl.ds(side * LANES, LANES)
                                ]

            store_lines(lines, matrix, out, z)
            return carry

        lax.fori_loop(0, DEPTH, layer, 0)


def place(me, slot_block, pieces):
    half = shape(5, DEPTH, 2, 4, ROWS, LANES)
    return pl.pallas_call(
        functools.partial(place_kernel, len(pieces)),
        out_shape=[half, half],
        in_specs=[spec_smem()] * 2 + [spec_vmem()] * len(pieces),
        out_specs=[spec_vmem()] * 2,
        scratch_shapes=[
            pltpu.VMEM((5, 2, 4 * ROWS, LANES), jnp.float32),
            one_hot_scratch(),
            pltpu.SMEM((len(pieces), HELD_MOST + 1), jnp.int32),
        ],
        compiler_params=params(),
        cost_estimate=cost(3),
        name="place",
    )(me, slot_block, *pieces)


def recover_kernel(levels_ref, before, low, high, after, out, state, s1, s2, s3, s4, lines, factors, matrix):
    one_hot(matrix, True)
    own_factors(factors, levels_ref, 0, 1.0)
    for number, part in enumerate((before, low, high, after)):
        copy_layers(part, 0, state, number * DEPTH, DEPTH)
    for number, dst in enumerate((s1, s2, s3, s4)):
        src = state if number == 0 else (s1, s2, s3)[number - 1]
        row = [factors[number, i] for i in range(17)]
        section(src, (0, 4), 1, state, 1 + number, dst, (0, 4), 0, 4 * DEPTH - 2 * (number + 1), row, True, False)

    def layer(z, carry):
        moved = None
        for parity in (0, 1):
            rows = s4[:, z, parity]
            rows = jnp.concatenate([rows[:1] + rows[4:], rows[1:]]).reshape(5 * 4 * ROWS, LANES)
            part = move_lanes(rows, matrix[parity])
            moved = part if moved is None else moved + part
        moved = moved.reshape(5, 4, ROWS, 2 * LANES)
        for field in range(5):
            for side in (0, 1):
                for line in range(4):
                    lines[field, side, pl.ds(line, ROWS, stride=4), :] = moved[
                        field, line, :, side * LANES : (side + 1) * LANES
                    ]
                out[field, z, :, pl.ds(side * LANES, LANES)] = lines[field, side]
        return carry

    lax.fori_loop(0, 2 * DEPTH, layer, 0)


def recover(levels, parts):
    buffer = lambda count: pltpu.VMEM((5, count, 2, 4, ROWS, LANES), jnp.float32)
    return pl.pallas_call(
        recover_kernel,
        out_shape=shape(5, 2 * DEPTH, 4 * ROWS, 2 * LANES),
        in_specs=[spec_smem()] + [spec_vmem()] * 4,
        out_specs=spec_vmem(),
        scratch_shapes=[buffer(count) for count in (16, 14, 12, 10, 8)]
        + [
            pltpu.VMEM((5, 2, 4 * ROWS, LANES), jnp.float32),
            pltpu.VMEM((4, 17, ROWS, LANES), jnp.float32),
            one_hot_scratch(),
        ],
        compiler_params=params(),
        cost_estimate=cost(10),
        name="recover",
    )(levels, *parts)


def after_all(*arrays):
    return lax.optimization_barrier(arrays)


def body(checkpoint, slot_block, live_state, levels, coefficients, tile_owner):
    groups = lax.axis_size("buddy")
    slabs = lax.axis_size("slab")
    me = lax.axis_index("buddy").astype(jnp.int32).reshape(1)
    tile_most = 2 * tile_owner.shape[1] // groups
    trade = lambda array, d: lax.ppermute(array, "buddy", [(i, i ^ d) for i in range(groups)])
    upward = lambda array: lax.ppermute(array, "slab", [(i, (i + 1) % slabs) for i in range(slabs)])
    downward = lambda array: lax.ppermute(array, "slab", [((i + 1) % slabs, i) for i in range(slabs)])

    facts = jnp.concatenate([levels.astype(jnp.float32).reshape(-1), coefficients.reshape(-1)])
    other_facts = [trade(facts, d) for d in range(1, groups)]
    low, high = prepare(checkpoint, live_state[0])
    before = upward(high)
    sent = gather_slots(me, slot_block, checkpoint, groups - 1)
    low, sent, other_facts = after_all(low, sent, other_facts)
    after = downward(low)
    middle = (groups // 2 - 1, groups // 2)
    received = [trade(sent[d - 1], d) for d in range(1, groups - 1)]
    received.append(
        lax.ppermute(sent[-1], "buddy", [(i, i ^ (groups - 1)) for i in range(groups) if i not in middle])
    )

    scalars = (me, slot_block, tile_owner, levels, coefficients, *other_facts)
    send_low, keep_low, *carries = half_step(first_half_kernel, scalars, (before, low, high), (), 3 * DEPTH, False)
    send_low, late, carries[0] = after_all(send_low, sent[-1], carries[0])
    arrived_low = trade(send_low, 1)
    received.append(lax.ppermute(late, "buddy", [middle, middle[::-1]]))
    send_high, keep_high = half_step(second_half_kernel, scalars, (after, high), carries, 2 * DEPTH, True)
    arrived_high = trade(send_high, 1)

    keep_high, received = after_all(keep_high, received)
    restored_low, restored_high = place(me, slot_block, received)
    restored_before = upward(restored_high)
    restored_after = downward(restored_low)
    shares = share(me, tile_owner, (keep_low, arrived_low, keep_high, arrived_high), groups)
    pieces = [shares[0]] + [trade(shares[d], d) for d in range(1, groups)]
    recovered = recover(levels, (restored_before, restored_low, restored_high, restored_after))
    recovered, pieces[0] = after_all(recovered, pieces[0])
    combined = collect(me, tile_owner, pieces, tile_most)
    return recovered[None], combined


def solution(mesh):
    return jax.shard_map(
        body,
        mesh=mesh,
        in_specs=(
            P("buddy", None, "slab", None, None),
            P(),
            P("buddy", None, "slab", None, None),
            P(None, "buddy", None),
            P(None, "buddy"),
            P("slab", None),
        ),
        out_specs=(P("buddy", None, "slab", None, None), P("buddy", None, "slab", None, None)),
        check_vma=False,
    )
```

```python
import functools

import jax
import jax.numpy as jnp
from jax import lax
from jax.experimental import pallas as pl
from jax.experimental.pallas import tpu as pltpu
from jax.sharding import PartitionSpec as P

VELOCITY = (0.3, -0.2, 0.45)
COURANT = 1.0
TILE_LINES = 2
HELD_MOST = 3
DEPTH = 4
LANES = 128
ROWS = 8


def spec_vmem():
    return pl.BlockSpec(memory_space=pltpu.VMEM)


def spec_smem():
    return pl.BlockSpec(memory_space=pltpu.SMEM)


def spec_any():
    return pl.BlockSpec(memory_space=pl.ANY)


def spec_hbm():
    return pl.BlockSpec(memory_space=pltpu.HBM)


def params(mebibytes):
    return pltpu.CompilerParams(vmem_limit_bytes=mebibytes * 1024 * 1024)


def cost(microseconds, flops=0):
    return pl.CostEstimate(flops=flops, bytes_accessed=microseconds, transcendentals=0)


def shape(*dims):
    return jax.ShapeDtypeStruct(dims, jnp.float32)


def add(*terms):
    total = None
    for term in terms:
        if term is not None:
            total = term if total is None else total + term
    return total


def sub(left, right):
    if right is None:
        return left
    return -right if left is None else left - right


def mul(factor, term):
    return None if term is None else factor * term


def lane_index():
    return lax.broadcasted_iota(jnp.int32, (ROWS, LANES), 1)


def turn_lanes(value, amount):
    return None if value is None else pltpu.roll(value, amount, 1)


def one_hot(out, join):
    row = lax.broadcasted_iota(jnp.int32, out.shape, 0)
    column = lax.broadcasted_iota(jnp.int32, out.shape, 1)
    if join:
        row, column = column, row
    out[...] = (column == row // 2 + LANES * (row % 2)).astype(jnp.float32).astype(jnp.bfloat16)


def move_lanes(rows, matrix):
    top = rows.astype(jnp.bfloat16)
    rest = rows - top.astype(jnp.float32)
    middle = rest.astype(jnp.bfloat16)
    low = (rest - middle.astype(jnp.float32)).astype(jnp.bfloat16)
    product = lambda part: jnp.dot(part, matrix, preferred_element_type=jnp.float32)
    return (product(top) + product(middle)) + product(low)


def one_hot_scratch():
    return pltpu.VMEM((2 * LANES, 2 * LANES), jnp.bfloat16)


def pick_rows(array, at):
    return jnp.take_along_axis(array, at, axis=0)


def direction_factors(axis_number):
    drift = VELOCITY[axis_number]
    wave = abs(drift) + 1.0
    carried = (0.5 * (wave - drift), 0.5 * (wave + drift))
    if drift >= 0:
        rising = (0.0, 0.5 * wave)
        falling = (0.5, 0.5 * drift)
    else:
        rising = (-0.5 * drift, 0.5)
        falling = (0.5 * wave, 0.0)
    return carried, rising, falling


def store_factors(out, spacing, weight):
    waves = [abs(drift) + 1.0 for drift in VELOCITY]
    spread = (waves[0] * spacing[0] + waves[1] * spacing[1]) + waves[2] * spacing[2]
    time_step = COURANT / spread
    for number, part in enumerate((4.0, 3.0, 2.0, 1.0)):
        scale = time_step * (1.0 / part)
        if number == 3:
            scale = scale * weight
        out[number, 0] = -(scale * spread)
        for axis_number in range(3):
            unit = scale * spacing[axis_number]
            carried, rising, falling = direction_factors(axis_number)
            one_sided = rising if 0.0 in rising else falling
            two_sided = falling if 0.0 in rising else rising
            for place, factor in enumerate((*carried, one_sided[0] + one_sided[1], *two_sided)):
                out[number, 1 + 5 * axis_number + place] = unit * factor
        out[number, 16] = weight


def splat(scalar):
    return jnp.full((ROWS, LANES), scalar, jnp.float32)


def spacing_of(level):
    return lax.shift_left(jnp.int32(1), level).astype(jnp.float32)


def own_factors(out, levels_ref, kind, weight):
    store_factors(out, [splat(spacing_of(levels_ref[kind, 0, axis])) for axis in range(3)], splat(weight))


def row_index():
    return lax.broadcasted_iota(jnp.int32, (ROWS, LANES), 0)


def by_slot(scalars):
    value = splat(scalars[0])
    for slot, scalar in enumerate(scalars[1:], 1):
        value = jnp.where(row_index() == slot, scalar, value)
    return value


def held_tables(me, block_ref, fact_refs, facts, factors, rows, masks):
    slots = block_ref.shape[1]
    for number, ref in enumerate(fact_refs):
        for item in range(3):
            facts[number, item] = spacing_of(ref[item].astype(jnp.int32))
        facts[number, 3] = ref[6]
    grids = [block_ref[me, slot] // slots for slot in range(slots)]
    places = [block_ref[me, slot] % slots for slot in range(slots)]
    numbers = [jnp.bitwise_xor(grid, me) - 1 for grid in grids]
    columns = [by_slot([facts[number, item] for number in numbers]) for item in range(4)]
    store_factors(factors, columns[:3], columns[3])
    for other in range(len(fact_refs)):
        for place, shift in enumerate((0, 1, -1)):
            at = jnp.zeros((ROWS, LANES), jnp.int32)
            mask = jnp.zeros((ROWS, LANES), jnp.float32)
            for slot in range(slots):
                target = jnp.where(numbers[slot] == other, (places[slot] + shift) % slots, -1)
                hit = row_index() == target
                at = jnp.where(hit, slot, at)
                mask = jnp.where(hit, 1.0, mask)
            rows[other, place] = at
            masks[other, place] = mask


def count_tiles(owner_ref, groups, start, amount, rank):
    for reader in range(groups):
        amount[reader] = 0
    for tile in range(owner_ref.shape[1]):
        reader = owner_ref[0, tile]
        rank[tile] = amount[reader]
        amount[reader] = amount[reader] + 1
    total = jnp.int32(0)
    for reader in range(groups):
        start[reader] = total
        total = total + amount[reader]


def tile_scratch(groups, tiles):
    return [pltpu.SMEM((groups,), jnp.int32), pltpu.SMEM((groups,), jnp.int32), pltpu.SMEM((tiles,), jnp.int32)]


def first_slot(start, kind):
    return (start + 1 - kind) // 2


def tile_tables(me, owner_ref, groups, counts, table):
    start, amount, rank = counts
    count_tiles(owner_ref, groups, start, amount, rank)
    kind = me % 2
    lists = [[jnp.zeros((ROWS, LANES), jnp.int32) for _ in range(2)] for _ in range(2)]
    for tile in range(owner_ref.shape[1]):
        position = start[owner_ref[0, tile]] + rank[tile]
        for number in (0, 1):
            mine = position % 2 == (kind if number == 1 else 1 - kind)
            hit = row_index() == jnp.where(mine, position // 2, -1)
            lists[number][0] = jnp.where(hit, tile // 2, lists[number][0])
            lists[number][1] = jnp.where(hit, tile % 2, lists[number][1])
    for number in (0, 1):
        for item in (0, 1):
            table[number, item] = lists[number][item]


def acoustic(axis_number, factors, rising_next, rising_prev, falling_next, falling_prev):
    one, two_next, two_prev = factors
    if VELOCITY[axis_number] >= 0:
        rising = mul(one, rising_prev)
        falling = add(mul(two_next, falling_next), mul(two_prev, falling_prev))
    else:
        rising = add(mul(two_next, rising_next), mul(two_prev, rising_prev))
        falling = mul(one, falling_next)
    return add(rising, falling), sub(rising, falling)


def section(src, src_lines, src_at, state, state_at, dst, dst_lines, dst_at, count, factors, wrap, scaled):
    def layer(number, carry):
        cache = {}

        def cell(field, parity, line, step=0):
            low, high = src_lines
            key = (field, parity, line, step)
            if key in cache:
                return cache[key]
            if low <= line < high:
                value = src[field, src_at + number + step, parity, line - low]
            elif wrap and line < low:
                value = pltpu.roll(cell(field, parity, high - 1), 1, 0)
            elif wrap:
                value = pltpu.roll(cell(field, parity, low), ROWS - 1, 0)
            else:
                value = None
            cache[key] = value
            return value

        def pair(axis_number, parity, line, step=0):
            key = ("pair", axis_number, parity, line, step)
            if key not in cache:
                pressure = cell(4, parity, line, step)
                speed = cell(1 + axis_number, parity, line, step)
                cache[key] = (None, None) if pressure is None else (pressure + speed, pressure - speed)
            return cache[key]

        centre = factors[0]
        for line in range(*dst_lines):
            for parity in (0, 1):
                result = [None] * 5
                for field in range(5):
                    terms = mul(centre, cell(field, parity, line))
                    if 0 <= line < 4:
                        held = state[field, state_at + number, parity, line]
                        terms = add(mul(factors[16], held) if scaled else held, terms)
                    result[field] = terms
                for axis_number in range(3):
                    forward, backward, *sound = factors[1 + 5 * axis_number : 6 + 5 * axis_number]

                    def neighbours(read):
                        if axis_number == 0:
                            other = read(1 - parity, line, 0)
                            if parity == 0:
                                return other, [turn_lanes(part, 1) for part in other]
                            return [turn_lanes(part, LANES - 1) for part in other], other
                        if axis_number == 1:
                            return read(parity, line + 1, 0), read(parity, line - 1, 0)
                        return read(parity, line, 1), read(parity, line, -1)

                    for field in range(4):
                        if field != 1 + axis_number:
                            (after,), (before,) = neighbours(
                                lambda *where, field=field: [cell(field, *where)]
                            )
                            result[field] = add(result[field], add(mul(forward, after), mul(backward, before)))
                    after, before = neighbours(lambda *where: pair(axis_number, *where))
                    pressure, speed = acoustic(
                        axis_number, sound, after[0], before[0], after[1], before[1]
                    )
                    result[4] = add(result[4], pressure)
                    result[1 + axis_number] = add(result[1 + axis_number], speed)
                for field in range(5):
                    dst[field, dst_at + number, parity, line - dst_lines[0]] = result[field]
        return carry

    lax.fori_loop(0, count, layer, 0)


def gather_slots_kernel(others, me_ref, block_ref, checkpoint, *outs):
    me = me_ref[0]
    slots = checkpoint.shape[0]
    grids = [block_ref[me, slot] // slots for slot in range(slots)]
    for slot in range(slots):
        rank = jnp.int32(0)
        for earlier in range(slot):
            rank = rank + (grids[earlier] == grids[slot]).astype(jnp.int32)
        for number in range(others):

            @pl.when(grids[slot] == jnp.bitwise_xor(me, number + 1))
            def _(slot=slot, number=number, rank=rank):
                def layer(z, carry):
                    for field in range(5):
                        outs[number][rank, field, z] = checkpoint[slot, field, z]
                    return carry

                lax.fori_loop(0, checkpoint.shape[2], layer, 0)


def gather_slots(me, slot_block, checkpoint, others):
    piece = shape(HELD_MOST, *checkpoint.shape[1:])
    return pl.pallas_call(
        functools.partial(gather_slots_kernel, others),
        out_shape=[piece] * others,
        in_specs=[spec_smem(), spec_smem(), spec_vmem()],
        out_specs=[spec_vmem()] * others,
        compiler_params=params(8),
        cost_estimate=cost(1),
        name="gather_slots",
    )(me, slot_block, checkpoint)


def store_lines(lines, matrix, out, z):
    halves = [lines[:, side].reshape(5 * 4 * ROWS, LANES) for side in (0, 1)]
    moved = move_lanes(jnp.concatenate(halves, axis=1), matrix[...]).reshape(5, 4, ROWS, 2 * LANES)
    for parity in (0, 1):
        lanes = slice(parity * LANES, (parity + 1) * LANES)
        out[0, z, parity] = moved[0, :, :, lanes] - moved[4, :, :, lanes]
        for field in range(1, 5):
            out[field, z, parity] = moved[field, :, :, lanes]


def prepare_kernel(half, firsts, checkpoint, live, *refs):
    out, held_lines, own_lines, matrix = refs[firsts:]
    slots = checkpoint.shape[0]
    one_hot(matrix, False)

    def layer(z, carry):
        for field in range(5):
            for side in (0, 1):
                lanes = pl.ds(side * LANES, LANES)
                for slot in range(slots):
                    held_lines[field, side, pl.ds(slot, 4, stride=ROWS), :] = checkpoint[
                        slot, field, half * DEPTH + z, :, lanes
                    ]
                for group in range(4):
                    rows = live[field, half * DEPTH + z, pl.ds(group * ROWS, ROWS), lanes]
                    for block in (0, 1):
                        own_lines[field, side, pl.ds(2 * group + block, 4, stride=ROWS), :] = rows[
                            4 * block : 4 * block + 4
                        ]
        store_lines(held_lines, matrix, out.at[0], z)
        store_lines(own_lines, matrix, out.at[1], z)
        return carry

    lax.fori_loop(0, DEPTH, layer, 0)


def prepare(half, checkpoint, live, firsts):
    lines = pltpu.VMEM((5, 2, 4 * ROWS, LANES), jnp.float32)
    return pl.pallas_call(
        functools.partial(prepare_kernel, half, len(firsts)),
        out_shape=shape(2, 5, DEPTH, 2, 4, ROWS, LANES),
        in_specs=[spec_vmem(), spec_vmem()] + [spec_any()] * len(firsts),
        out_specs=spec_vmem(),
        scratch_shapes=[lines, lines, one_hot_scratch()],
        compiler_params=params(8),
        cost_estimate=cost(1),
        name="prepare",
    )(checkpoint, live, *firsts)


HELD_LINES = ((0, 4), (-1, 5), (-2, 6), (-3, 7), (-4, 8))
LIVE_LINES = ((0, 4),) * 5
CARRIES = ((0, 6), (0, 8), (0, 10), (1, 4), (1, 4), (1, 4))


def copy_layers(src, src_at, dst, dst_at, count):
    def layer(z, carry):
        dst[:, dst_at + z] = src[:, src_at + z]
        return carry

    lax.fori_loop(0, count, layer, 0)


def weigh_and_pack(others, held_out, live_out, rows_ref, mask_ref, tiles_ref, send, keep):
    def layer(z, carry):
        for field in (4, 0, 1, 2, 3):
            for parity in (0, 1):
                total = [live_out[field, z, parity, line] for line in range(4)]
                for other in range(others):
                    for place, first in ((0, 4), (1, 8), (2, 0)):
                        at = rows_ref[other, place]
                        mask = mask_ref[other, place]
                        for line in range(4):
                            image = held_out[field, z, parity, first + line]
                            total[line] = total[line] + mask * pick_rows(image, at)
                for number, out in ((0, send), (1, keep)):
                    at = tiles_ref[number, 0]
                    lower = tiles_ref[number, 1] == 0
                    for line in (0, 1):
                        value = jnp.where(lower, pick_rows(total[line], at), pick_rows(total[2 + line], at))
                        if field == 0:
                            value = value + out[4, z, parity, line]
                        out[field, z, parity, line] = value
        return carry

    lax.fori_loop(0, DEPTH, layer, 0)


def half_tables(others, scalars, scratch):
    me_ref, block_ref, owner_ref, levels_ref, weights_ref, *fact_refs = scalars
    live_factors, held_factors, rows, masks, tiles, facts, *counts = scratch
    me = me_ref[0]
    own_factors(live_factors, levels_ref, 1, weights_ref[1, 0])
    held_tables(me, block_ref, fact_refs, facts, held_factors, rows, masks)
    tile_tables(me, owner_ref, others + 1, counts, tiles)
    return live_factors, held_factors, rows, masks, tiles


def start_halo(part, held, live, at, sems):
    copies = [
        pltpu.make_async_copy(part.at[kind], state.at[:, pl.ds(at, DEPTH)], sems.at[kind])
        for kind, state in ((0, held), (1, live))
    ]
    for copy in copies:
        copy.start()
    return copies


def first_half_kernel(others, *refs):
    scalars, refs = refs[: 5 + others], refs[5 + others :]
    before, low, high, send, keep, *refs = refs
    carries, refs = refs[:6], refs[6:]
    held, live, h1, h2, h3, h4, l1, l2, l3, l4, sems, *scratch = refs
    waiting = start_halo(before, held, live, 0, sems)
    for kind, state in ((0, held), (1, live)):
        for number, part in ((1, low), (2, high)):
            copy_layers(part.at[kind], 0, state, number * DEPTH, DEPTH)
    live_factors, held_factors, rows, masks, tiles = half_tables(others, scalars, scratch)
    waiting[0].wait()
    run_sections(held, (h1, h2, h3, h4), HELD_LINES, False, held_factors, False)
    waiting[1].wait()
    run_sections(live, (l1, l2, l3, l4), LIVE_LINES, True, live_factors, False)
    last = ((h1, 8), (h2, 6), (h3, 4), (l1, 8), (l2, 6), (l3, 4))
    for (src, at), out in zip(last, carries):
        copy_layers(src, at, out, 0, 2)
    weigh_and_pack(others, h4, l4, rows, masks, tiles, send, keep)


def second_half_kernel(others, *refs):
    scalars, refs = refs[: 5 + others], refs[5 + others :]
    after, high, _, *refs = refs
    carries, (send, keep, *refs) = refs[:6], refs[6:]
    held, live, h1, h2, h3, h4, l1, l2, l3, l4, sems, *scratch = refs
    waiting = start_halo(after, held, live, DEPTH, sems)
    for kind, state in ((0, held), (1, live)):
        copy_layers(high.at[kind], 0, state, 0, DEPTH)
    for carry, dst in zip(carries, (h1, h2, h3, l1, l2, l3)):
        copy_layers(carry, 0, dst, 0, 2)
    live_factors, held_factors, rows, masks, tiles = half_tables(others, scalars, scratch)
    waiting[0].wait()
    run_sections(held, (h1, h2, h3, h4), HELD_LINES, False, held_factors, True)
    waiting[1].wait()
    run_sections(live, (l1, l2, l3, l4), LIVE_LINES, True, live_factors, True)
    weigh_and_pack(others, h4, l4, rows, masks, tiles, send, keep)


def run_sections(state, stages, lines, wrap, factors, continued):
    for number in range(4):
        row = [factors[number, i] for i in range(17)]
        src = state if number == 0 else stages[number - 1]
        if continued:
            src_at = 3 if number == 0 else 1
            state_at = 3 - number
            dst_at, count = (0 if number == 3 else 2), DEPTH
        else:
            src_at, state_at, dst_at, count = 1, 1 + number, 0, 3 * DEPTH - 2 * (number + 1)
        section(
            src, lines[number], src_at, state, state_at, stages[number], lines[number + 1], dst_at,
            count, row, wrap, number == 3,
        )


def half_step(kernel, scalars, parts, carries_in, layers, last):
    others = len(scalars) - 5
    tiles = scalars[2].shape[1]
    packed = shape(5, DEPTH, 2, 2, ROWS, LANES)
    buffer = lambda count, lines: pltpu.VMEM((5, count, 2, lines, ROWS, LANES), jnp.float32)
    table = lambda *dims, kind=jnp.float32: pltpu.VMEM((*dims, ROWS, LANES), kind)
    carry_shapes = [shape(5, 2, 2, lines, ROWS, LANES) for lines in (6, 8, 10, 4, 4, 4)]
    outs = [packed, packed] + ([] if last else carry_shapes)
    stage_layers = (6, 6, 6, DEPTH) if last else (10, 8, 6, DEPTH)
    return pl.pallas_call(
        functools.partial(kernel, others),
        out_shape=outs,
        in_specs=[spec_smem()] * len(scalars) + [spec_any()] + [spec_vmem()] * (len(parts) - 1 + len(carries_in)),
        out_specs=[spec_vmem()] * len(outs),
        scratch_shapes=[buffer(layers, 4), buffer(layers, 4)]
        + [buffer(count, lines) for count, lines in zip(stage_layers, (6, 8, 10, 12))]
        + [buffer(count, 4) for count in stage_layers]
        + [pltpu.SemaphoreType.DMA((2,))]
        + [table(4, 17), table(4, 17), table(others, 3, kind=jnp.int32), table(others, 3), table(2, 2, kind=jnp.int32)]
        + [pltpu.SMEM((others, 4), jnp.float32)]
        + tile_scratch(others + 1, tiles),
        compiler_params=params(24),
        cost_estimate=cost(8 if last else 12),
        name="second_half" if last else "first_half",
    )(*scalars, *parts, *carries_in)


def after_kernel(count, *refs):
    refs[count][...] = jnp.zeros((ROWS, LANES), jnp.float32)


def there(arrays):
    return pl.pallas_call(
        functools.partial(after_kernel, len(arrays)),
        out_shape=shape(ROWS, LANES),
        in_specs=[spec_any()] * len(arrays),
        out_specs=spec_vmem(),
        compiler_params=params(1),
        cost_estimate=cost(1, 10**12),
        name="there",
    )(*arrays)


def share_kernel(groups, me_ref, owner_ref, keep_low, arrived_low, keep_high, arrived_high, *refs):
    outs, (table, *counts) = refs[:groups], refs[groups:]
    start = counts[0]
    count_tiles(owner_ref, groups, *counts)
    me = me_ref[0]
    for number in range(groups):
        first = first_slot(start[jnp.bitwise_xor(me, number)], me % 2)
        table[number] = jnp.minimum(first + row_index() // 2, ROWS - 1)

    for half, keep, arrived in ((0, keep_low, arrived_low), (1, keep_high, arrived_high)):

        def layer(z, carry, half=half, keep=keep, arrived=arrived):
            odd = row_index() % 2 == 1
            for field in range(5):
                for parity in (0, 1):
                    first = keep[field, z, parity, 0] + arrived[field, z, parity, 0]
                    second = keep[field, z, parity, 1] + arrived[field, z, parity, 1]
                    for number in range(groups):
                        at = table[number]
                        outs[number][field, half * DEPTH + z, parity] = jnp.where(
                            odd, pick_rows(second, at), pick_rows(first, at)
                        )
            return carry

        lax.fori_loop(0, DEPTH, layer, 0)


def share(me, owner, halves, groups):
    piece = shape(5, 2 * DEPTH, 2, ROWS, LANES)
    return pl.pallas_call(
        functools.partial(share_kernel, groups),
        out_shape=[piece] * groups,
        in_specs=[spec_smem()] * 2 + [spec_vmem()] * len(halves),
        out_specs=[spec_vmem()] * groups,
        scratch_shapes=[pltpu.VMEM((groups, ROWS, LANES), jnp.int32)] + tile_scratch(groups, owner.shape[1]),
        compiler_params=params(8),
        cost_estimate=cost(1),
        name="share",
    )(me, owner, *halves)


def collect_kernel(groups, tile_most, me_ref, owner_ref, *rest):
    pieces, (result, out, sems, matrix, *counts) = rest[:groups], rest[groups:]
    count_tiles(owner_ref, groups, *counts)
    one_hot(matrix, True)
    me = me_ref[0]
    mine = counts[1][me]
    swap = counts[0][me] % 2 != me % 2

    def layer(z, carry):
        even = 2 * (row_index() // 2) < mine
        odd = 2 * (row_index() // 2) + 1 < mine
        halves = []
        for parity in (0, 1):
            sums = []
            for kind in (0, 1):
                value = pieces[kind][:, z, parity]
                for other in range(2 + kind, groups, 2):
                    value = value + pieces[other][:, z, parity]
                sums.append(value)
            rows = jnp.concatenate(
                [
                    jnp.where(even, jnp.where(swap, sums[1], sums[0]), 0.0),
                    jnp.where(odd, jnp.where(swap, sums[0], sums[1]), 0.0),
                ]
            )
            halves.append(rows.reshape(10 * ROWS, LANES))
        moved = move_lanes(jnp.concatenate(halves, axis=1), matrix[...]).reshape(2, 5, ROWS, 2 * LANES)
        for kind in (0, 1):
            for field in range(5):
                for slot in range(tile_most // 2):
                    out[2 * slot + kind, field, z] = moved[kind, field, 2 * slot : 2 * slot + 2]
        return carry

    copies = []
    for part in range(4):
        lax.fori_loop(2 * part, 2 * part + 2, layer, 0)
        layers = pl.ds(2 * part, 2)
        copies.append(pltpu.make_async_copy(out.at[:, :, layers], result.at[:, :, layers], sems.at[part]))
        copies[part].start()
    for copy in copies:
        copy.wait()


def collect(me, owner, pieces, tile_most):
    groups = len(pieces)
    dims = (tile_most, 5, 2 * DEPTH, TILE_LINES, 2 * LANES)
    return pl.pallas_call(
        functools.partial(collect_kernel, groups, tile_most),
        out_shape=shape(*dims),
        in_specs=[spec_smem()] * 2 + [spec_vmem()] * len(pieces),
        out_specs=spec_any(),
        scratch_shapes=[pltpu.VMEM(dims, jnp.float32), pltpu.SemaphoreType.DMA((4,)), one_hot_scratch()]
        + tile_scratch(groups, owner.shape[1]),
        compiler_params=params(8),
        cost_estimate=cost(2),
        name="collect",
    )(me, owner, *pieces)


def place_kernel(others, me_ref, block_ref, *rest):
    pieces, (low, high, lines, matrix, table) = rest[:others], rest[others:]
    one_hot(matrix, False)
    me = me_ref[0]
    slots = block_ref.shape[1]
    groups = block_ref.shape[0]
    inner = (me == groups // 2 - 1) | (me == groups // 2)
    for number in range(others):
        for slot in range(HELD_MOST):
            table[number, slot] = -1
        holder = jnp.bitwise_xor(me, min(number + 1, groups - 1))
        rank = jnp.int32(0)
        for slot in range(slots):
            block = block_ref[holder, slot]
            mine = block // slots == me
            if number >= groups - 2:
                mine = mine & (inner if number == groups - 1 else jnp.logical_not(inner))
            table[number, jnp.where(mine, rank, HELD_MOST)] = block % slots
            rank = rank + mine.astype(jnp.int32)
    for half, out in ((0, low), (1, high)):

        def layer(z, carry, half=half, out=out):
            for number in range(others):
                for slot in range(HELD_MOST):
                    block = table[number, slot]

                    @pl.when(block >= 0)
                    def _(number=number, slot=slot, block=block):
                        for field in range(5):
                            for side in (0, 1):
                                lines[field, side, pl.ds(block, 4, stride=ROWS), :] = pieces[number][
                                    slot, field, half * DEPTH + z, :, pl.ds(side * LANES, LANES)
                                ]

            store_lines(lines, matrix, out, z)
            return carry

        lax.fori_loop(0, DEPTH, layer, 0)


def place(me, slot_block, pieces):
    half = shape(5, DEPTH, 2, 4, ROWS, LANES)
    return pl.pallas_call(
        functools.partial(place_kernel, len(pieces)),
        out_shape=[half, half],
        in_specs=[spec_smem()] * 2 + [spec_vmem()] * len(pieces),
        out_specs=[spec_vmem()] * 2,
        scratch_shapes=[
            pltpu.VMEM((5, 2, 4 * ROWS, LANES), jnp.float32),
            one_hot_scratch(),
            pltpu.SMEM((len(pieces), HELD_MOST + 1), jnp.int32),
        ],
        compiler_params=params(8),
        cost_estimate=cost(3),
        name="place",
    )(me, slot_block, *pieces)


def recover_kernel(levels_ref, before, low, high, after, result, state, s1, s2, s3, s4, out, lines, factors, matrix, sems):
    one_hot(matrix, True)
    own_factors(factors, levels_ref, 0, 1.0)
    for number, part in enumerate((before, low, high, after)):
        copy_layers(part, 0, state, number * DEPTH, DEPTH)
    for number, dst in enumerate((s1, s2, s3, s4)):
        src = state if number == 0 else (s1, s2, s3)[number - 1]
        row = [factors[number, i] for i in range(17)]
        section(src, (0, 4), 1, state, 1 + number, dst, (0, 4), 0, 4 * DEPTH - 2 * (number + 1), row, True, False)

    def layer(z, carry):
        halves = []
        for parity in (0, 1):
            rows = s4[:, z, parity]
            halves.append(jnp.concatenate([rows[:1] + rows[4:], rows[1:]]).reshape(5 * 4 * ROWS, LANES))
        moved = move_lanes(jnp.concatenate(halves, axis=1), matrix[...]).reshape(5, 4, ROWS, 2 * LANES)
        for field in range(5):
            for side in (0, 1):
                for line in range(4):
                    lines[field, side, pl.ds(line, ROWS, stride=4), :] = moved[
                        field, line, :, side * LANES : (side + 1) * LANES
                    ]
                out[field, z, :, pl.ds(side * LANES, LANES)] = lines[field, side]
        pltpu.make_async_copy(out.at[:, z], result.at[:, z], sems.at[z]).start()
        return carry

    lax.fori_loop(0, 2 * DEPTH, layer, 0)
    for z in range(2 * DEPTH):
        pltpu.make_async_copy(out.at[:, z], result.at[:, z], sems.at[z]).wait()


def recover(levels, parts):
    buffer = lambda count: pltpu.VMEM((5, count, 2, 4, ROWS, LANES), jnp.float32)
    return pl.pallas_call(
        recover_kernel,
        out_shape=shape(5, 2 * DEPTH, 4 * ROWS, 2 * LANES),
        in_specs=[spec_smem()] + [spec_vmem()] * 4,
        out_specs=spec_any(),
        scratch_shapes=[buffer(count) for count in (16, 14, 12, 10, 8)]
        + [
            pltpu.VMEM((5, 2 * DEPTH, 4 * ROWS, 2 * LANES), jnp.float32),
            pltpu.VMEM((5, 2, 4 * ROWS, LANES), jnp.float32),
            pltpu.VMEM((4, 17, ROWS, LANES), jnp.float32),
            one_hot_scratch(),
            pltpu.SemaphoreType.DMA((2 * DEPTH,)),
        ],
        compiler_params=params(20),
        cost_estimate=cost(10),
        name="recover",
    )(levels, *parts)


def after_all(*arrays):
    return lax.optimization_barrier(arrays)


def body(checkpoint, slot_block, live_state, levels, coefficients, tile_owner):
    groups = lax.axis_size("buddy")
    slabs = lax.axis_size("slab")
    me = lax.axis_index("buddy").astype(jnp.int32).reshape(1)
    tile_most = 2 * tile_owner.shape[1] // groups
    trade = lambda array, d: lax.ppermute(array, "buddy", [(i, i ^ d) for i in range(groups)])
    upward = lambda array: lax.ppermute(array, "slab", [(i, (i + 1) % slabs) for i in range(slabs)])
    downward = lambda array: lax.ppermute(array, "slab", [((i + 1) % slabs, i) for i in range(slabs)])

    facts = jnp.concatenate([levels.astype(jnp.float32).reshape(-1), coefficients.reshape(-1)])
    other_facts = [trade(facts, d) for d in range(1, groups)]
    high = prepare(1, checkpoint, live_state[0], ())
    before = upward(high)
    sent = gather_slots(me, slot_block, checkpoint, groups - 1)
    sent, other_facts = after_all(sent, other_facts)
    low = prepare(0, checkpoint, live_state[0], other_facts)
    after = downward(low)
    middle = (groups // 2 - 1, groups // 2)
    received = [trade(sent[d - 1], d) for d in range(1, groups - 1)]
    received.append(
        lax.ppermute(sent[-1], "buddy", [(i, i ^ (groups - 1)) for i in range(groups) if i not in middle])
    )

    scalars = (me, slot_block, tile_owner, levels, coefficients, *other_facts)
    send_low, keep_low, *carries = half_step(first_half_kernel, scalars, (before, low, high), (), 3 * DEPTH, False)
    send_low, late, carries[0] = after_all(send_low, sent[-1], carries[0])
    arrived_low = trade(send_low, 1)
    received.append(lax.ppermute(late, "buddy", [middle, middle[::-1]]))
    send_high, keep_high = half_step(second_half_kernel, scalars, (after, high, there(received[:-1])), carries, 2 * DEPTH, True)
    arrived_high = trade(send_high, 1)

    keep_high, received = after_all(keep_high, received)
    restored_low, restored_high = place(me, slot_block, received)
    restored_before = upward(restored_high)
    restored_after = downward(restored_low)
    shares = share(me, tile_owner, (keep_low, arrived_low, keep_high, arrived_high), groups)
    pieces = [shares[0]] + [trade(shares[d], d) for d in range(groups - 1, 0, -1)][::-1]
    recovered = recover(levels, (restored_before, restored_low, restored_high, restored_after))
    recovered, pieces[0] = after_all(recovered, pieces[0])
    combined = collect(me, tile_owner, pieces, tile_most)
    return recovered[None], combined


def solution(mesh):
    return jax.shard_map(
        body,
        mesh=mesh,
        in_specs=(
            P("buddy", None, "slab", None, None),
            P(),
            P("buddy", None, "slab", None, None),
            P(None, "buddy", None),
            P(None, "buddy"),
            P("slab", None),
        ),
        out_specs=(P("buddy", None, "slab", None, None), P("buddy", None, "slab", None, None)),
        check_vma=False,
    )
```

```python
import functools

import jax
import jax.numpy as jnp
from jax import lax
from jax.experimental import pallas as pl
from jax.experimental.pallas import tpu as pltpu
from jax.sharding import PartitionSpec as P

VELOCITY = (0.3, -0.2, 0.45)
COURANT = 1.0
TILE_LINES = 2
HELD_MOST = 3
DEPTH = 4
LANES = 128
ROWS = 8


def spec_vmem():
    return pl.BlockSpec(memory_space=pltpu.VMEM)


def spec_smem():
    return pl.BlockSpec(memory_space=pltpu.SMEM)


def spec_any():
    return pl.BlockSpec(memory_space=pl.ANY)


def spec_hbm():
    return pl.BlockSpec(memory_space=pltpu.HBM)


def params(mebibytes):
    return pltpu.CompilerParams(vmem_limit_bytes=mebibytes * 1024 * 1024)


def cost(microseconds, flops=0):
    return pl.CostEstimate(flops=flops, bytes_accessed=microseconds, transcendentals=0)


def shape(*dims):
    return jax.ShapeDtypeStruct(dims, jnp.float32)


def add(*terms):
    total = None
    for term in terms:
        if term is not None:
            total = term if total is None else total + term
    return total


def sub(left, right):
    if right is None:
        return left
    return -right if left is None else left - right


def mul(factor, term):
    return None if term is None else factor * term


def lane_index():
    return lax.broadcasted_iota(jnp.int32, (ROWS, LANES), 1)


def turn_lanes(value, amount):
    return None if value is None else pltpu.roll(value, amount, 1)


def one_hot(out, join):
    row = lax.broadcasted_iota(jnp.int32, out.shape, 0)
    column = lax.broadcasted_iota(jnp.int32, out.shape, 1)
    if join:
        row, column = column, row
    out[...] = (column == row // 2 + LANES * (row % 2)).astype(jnp.float32).astype(jnp.bfloat16)


def move_lanes(rows, matrix):
    top = rows.astype(jnp.bfloat16)
    rest = rows - top.astype(jnp.float32)
    middle = rest.astype(jnp.bfloat16)
    low = (rest - middle.astype(jnp.float32)).astype(jnp.bfloat16)
    product = lambda part: jnp.dot(part, matrix, preferred_element_type=jnp.float32)
    return (product(top) + product(middle)) + product(low)


def one_hot_scratch():
    return pltpu.VMEM((2 * LANES, 2 * LANES), jnp.bfloat16)


def pick_rows(array, at):
    return jnp.take_along_axis(array, at, axis=0)


def direction_factors(axis_number):
    drift = VELOCITY[axis_number]
    wave = abs(drift) + 1.0
    carried = (0.5 * (wave - drift), 0.5 * (wave + drift))
    if drift >= 0:
        rising = (0.0, 0.5 * wave)
        falling = (0.5, 0.5 * drift)
    else:
        rising = (-0.5 * drift, 0.5)
        falling = (0.5 * wave, 0.0)
    return carried, rising, falling


def store_factors(out, spacing, weight):
    waves = [abs(drift) + 1.0 for drift in VELOCITY]
    spread = (waves[0] * spacing[0] + waves[1] * spacing[1]) + waves[2] * spacing[2]
    time_step = COURANT / spread
    for number, part in enumerate((4.0, 3.0, 2.0, 1.0)):
        scale = time_step * (1.0 / part)
        if number == 3:
            scale = scale * weight
        out[number, 0] = -(scale * spread)
        for axis_number in range(3):
            unit = scale * spacing[axis_number]
            carried, rising, falling = direction_factors(axis_number)
            one_sided = rising if 0.0 in rising else falling
            two_sided = falling if 0.0 in rising else rising
            for place, factor in enumerate((*carried, one_sided[0] + one_sided[1], *two_sided)):
                out[number, 1 + 5 * axis_number + place] = unit * factor
        out[number, 16] = weight


def splat(scalar):
    return jnp.full((ROWS, LANES), scalar, jnp.float32)


def spacing_of(level):
    return lax.shift_left(jnp.int32(1), level).astype(jnp.float32)


def own_factors(out, levels_ref, kind, weight):
    store_factors(out, [splat(spacing_of(levels_ref[kind, 0, axis])) for axis in range(3)], splat(weight))


def row_index():
    return lax.broadcasted_iota(jnp.int32, (ROWS, LANES), 0)


def by_slot(scalars):
    value = splat(scalars[0])
    for slot, scalar in enumerate(scalars[1:], 1):
        value = jnp.where(row_index() == slot, scalar, value)
    return value


def held_tables(me, block_ref, fact_refs, facts, factors, rows, masks):
    slots = block_ref.shape[1]
    for number, ref in enumerate(fact_refs):
        for item in range(3):
            facts[number, item] = spacing_of(ref[item].astype(jnp.int32))
        facts[number, 3] = ref[6]
    grids = [block_ref[me, slot] // slots for slot in range(slots)]
    places = [block_ref[me, slot] % slots for slot in range(slots)]
    numbers = [jnp.bitwise_xor(grid, me) - 1 for grid in grids]
    columns = [by_slot([facts[number, item] for number in numbers]) for item in range(4)]
    store_factors(factors, columns[:3], columns[3])
    for other in range(len(fact_refs)):
        for place, shift in enumerate((0, 1, -1)):
            at = jnp.zeros((ROWS, LANES), jnp.int32)
            mask = jnp.zeros((ROWS, LANES), jnp.float32)
            for slot in range(slots):
                target = jnp.where(numbers[slot] == other, (places[slot] + shift) % slots, -1)
                hit = row_index() == target
                at = jnp.where(hit, slot, at)
                mask = jnp.where(hit, 1.0, mask)
            rows[other, place] = at
            masks[other, place] = mask


def count_tiles(owner_ref, groups, start, amount, rank):
    for reader in range(groups):
        amount[reader] = 0
    for tile in range(owner_ref.shape[1]):
        reader = owner_ref[0, tile]
        rank[tile] = amount[reader]
        amount[reader] = amount[reader] + 1
    total = jnp.int32(0)
    for reader in range(groups):
        start[reader] = total
        total = total + amount[reader]


def tile_scratch(groups, tiles):
    return [pltpu.SMEM((groups,), jnp.int32), pltpu.SMEM((groups,), jnp.int32), pltpu.SMEM((tiles,), jnp.int32)]


def first_slot(start, kind):
    return (start + 1 - kind) // 2


def tile_tables(me, owner_ref, groups, counts, table):
    start, amount, rank = counts
    count_tiles(owner_ref, groups, start, amount, rank)
    kind = me % 2
    lists = [[jnp.zeros((ROWS, LANES), jnp.int32) for _ in range(2)] for _ in range(2)]
    for tile in range(owner_ref.shape[1]):
        position = start[owner_ref[0, tile]] + rank[tile]
        for number in (0, 1):
            mine = position % 2 == (kind if number == 1 else 1 - kind)
            hit = row_index() == jnp.where(mine, position // 2, -1)
            lists[number][0] = jnp.where(hit, tile // 2, lists[number][0])
            lists[number][1] = jnp.where(hit, tile % 2, lists[number][1])
    for number in (0, 1):
        for item in (0, 1):
            table[number, item] = lists[number][item]


def acoustic(axis_number, factors, rising_next, rising_prev, falling_next, falling_prev):
    one, two_next, two_prev = factors
    if VELOCITY[axis_number] >= 0:
        rising = mul(one, rising_prev)
        falling = add(mul(two_next, falling_next), mul(two_prev, falling_prev))
    else:
        rising = add(mul(two_next, rising_next), mul(two_prev, rising_prev))
        falling = mul(one, falling_next)
    return add(rising, falling), sub(rising, falling)


def section(src, src_lines, src_at, state, state_at, dst, dst_lines, dst_at, count, factors, wrap, scaled):
    def layer(number, carry):
        cache = {}

        def cell(field, parity, line, step=0):
            low, high = src_lines
            key = (field, parity, line, step)
            if key in cache:
                return cache[key]
            if low <= line < high:
                value = src[field, src_at + number + step, parity, line - low]
            elif wrap and line < low:
                value = pltpu.roll(cell(field, parity, high - 1), 1, 0)
            elif wrap:
                value = pltpu.roll(cell(field, parity, low), ROWS - 1, 0)
            else:
                value = None
            cache[key] = value
            return value

        def pair(axis_number, parity, line, step=0):
            key = ("pair", axis_number, parity, line, step)
            if key not in cache:
                pressure = cell(4, parity, line, step)
                speed = cell(1 + axis_number, parity, line, step)
                cache[key] = (None, None) if pressure is None else (pressure + speed, pressure - speed)
            return cache[key]

        centre = factors[0]
        for line in range(*dst_lines):
            for parity in (0, 1):
                result = [None] * 5
                for field in range(5):
                    terms = mul(centre, cell(field, parity, line))
                    if 0 <= line < 4:
                        held = state[field, state_at + number, parity, line]
                        terms = add(mul(factors[16], held) if scaled else held, terms)
                    result[field] = terms
                for axis_number in range(3):
                    forward, backward, *sound = factors[1 + 5 * axis_number : 6 + 5 * axis_number]

                    def neighbours(read):
                        if axis_number == 0:
                            other = read(1 - parity, line, 0)
                            if parity == 0:
                                return other, [turn_lanes(part, 1) for part in other]
                            return [turn_lanes(part, LANES - 1) for part in other], other
                        if axis_number == 1:
                            return read(parity, line + 1, 0), read(parity, line - 1, 0)
                        return read(parity, line, 1), read(parity, line, -1)

                    for field in range(4):
                        if field != 1 + axis_number:
                            (after,), (before,) = neighbours(
                                lambda *where, field=field: [cell(field, *where)]
                            )
                            result[field] = add(result[field], add(mul(forward, after), mul(backward, before)))
                    after, before = neighbours(lambda *where: pair(axis_number, *where))
                    pressure, speed = acoustic(
                        axis_number, sound, after[0], before[0], after[1], before[1]
                    )
                    result[4] = add(result[4], pressure)
                    result[1 + axis_number] = add(result[1 + axis_number], speed)
                for field in range(5):
                    dst[field, dst_at + number, parity, line - dst_lines[0]] = result[field]
        return carry

    lax.fori_loop(0, count, layer, 0)


def gather_slots_kernel(others, me_ref, block_ref, checkpoint, *outs):
    me = me_ref[0]
    slots = checkpoint.shape[0]
    grids = [block_ref[me, slot] // slots for slot in range(slots)]
    for slot in range(slots):
        rank = jnp.int32(0)
        for earlier in range(slot):
            rank = rank + (grids[earlier] == grids[slot]).astype(jnp.int32)
        for number in range(others):

            @pl.when(grids[slot] == jnp.bitwise_xor(me, number + 1))
            def _(slot=slot, number=number, rank=rank):
                def layer(z, carry):
                    for field in range(5):
                        outs[number][rank, field, z] = checkpoint[slot, field, z]
                    return carry

                lax.fori_loop(0, checkpoint.shape[2], layer, 0)


def gather_slots(me, slot_block, checkpoint, others):
    piece = shape(HELD_MOST, *checkpoint.shape[1:])
    return pl.pallas_call(
        functools.partial(gather_slots_kernel, others),
        out_shape=[piece] * others,
        in_specs=[spec_smem(), spec_smem(), spec_vmem()],
        out_specs=[spec_vmem()] * others,
        compiler_params=params(8),
        cost_estimate=cost(1),
        name="gather_slots",
    )(me, slot_block, checkpoint)


def store_lines(lines, matrix, out, z):
    halves = [lines[:, side].reshape(5 * 4 * ROWS, LANES) for side in (0, 1)]
    moved = move_lanes(jnp.concatenate(halves, axis=1), matrix[...]).reshape(5, 4, ROWS, 2 * LANES)
    for parity in (0, 1):
        lanes = slice(parity * LANES, (parity + 1) * LANES)
        out[0, z, parity] = moved[0, :, :, lanes] - moved[4, :, :, lanes]
        for field in range(1, 5):
            out[field, z, parity] = moved[field, :, :, lanes]


def prepare_kernel(half, firsts, checkpoint, live, *refs):
    out, held_lines, own_lines, matrix = refs[firsts:]
    slots = checkpoint.shape[0]
    one_hot(matrix, False)

    def layer(z, carry):
        for field in range(5):
            for side in (0, 1):
                lanes = pl.ds(side * LANES, LANES)
                for slot in range(slots):
                    held_lines[field, side, pl.ds(slot, 4, stride=ROWS), :] = checkpoint[
                        slot, field, half * DEPTH + z, :, lanes
                    ]
                for group in range(4):
                    rows = live[field, half * DEPTH + z, pl.ds(group * ROWS, ROWS), lanes]
                    for block in (0, 1):
                        own_lines[field, side, pl.ds(2 * group + block, 4, stride=ROWS), :] = rows[
                            4 * block : 4 * block + 4
                        ]
        store_lines(held_lines, matrix, out.at[0], z)
        store_lines(own_lines, matrix, out.at[1], z)
        return carry

    lax.fori_loop(0, DEPTH, layer, 0)


def prepare(half, checkpoint, live, firsts):
    lines = pltpu.VMEM((5, 2, 4 * ROWS, LANES), jnp.float32)
    return pl.pallas_call(
        functools.partial(prepare_kernel, half, len(firsts)),
        out_shape=shape(2, 5, DEPTH, 2, 4, ROWS, LANES),
        in_specs=[spec_vmem(), spec_vmem()] + [spec_any()] * len(firsts),
        out_specs=spec_vmem(),
        scratch_shapes=[lines, lines, one_hot_scratch()],
        compiler_params=params(8),
        cost_estimate=cost(1),
        name="prepare",
    )(checkpoint, live, *firsts)


HELD_LINES = ((0, 4), (-1, 5), (-2, 6), (-3, 7), (-4, 8))
LIVE_LINES = ((0, 4),) * 5
CARRIES = ((0, 6), (0, 8), (0, 10), (1, 4), (1, 4), (1, 4))


def copy_layers(src, src_at, dst, dst_at, count):
    def layer(z, carry):
        dst[:, dst_at + z] = src[:, src_at + z]
        return carry

    lax.fori_loop(0, count, layer, 0)


def weigh_and_pack(others, held_out, live_out, rows_ref, mask_ref, tiles_ref, send, keep):
    def layer(z, carry):
        for field in (4, 0, 1, 2, 3):
            for parity in (0, 1):
                total = [live_out[field, z, parity, line] for line in range(4)]
                for other in range(others):
                    for place, first in ((0, 4), (1, 8), (2, 0)):
                        at = rows_ref[other, place]
                        mask = mask_ref[other, place]
                        for line in range(4):
                            image = held_out[field, z, parity, first + line]
                            total[line] = total[line] + mask * pick_rows(image, at)
                for number, out in ((0, send), (1, keep)):
                    at = tiles_ref[number, 0]
                    lower = tiles_ref[number, 1] == 0
                    for line in (0, 1):
                        value = jnp.where(lower, pick_rows(total[line], at), pick_rows(total[2 + line], at))
                        if field == 0:
                            value = value + out[4, z, parity, line]
                        out[field, z, parity, line] = value
        return carry

    lax.fori_loop(0, DEPTH, layer, 0)


def half_tables(others, scalars, scratch):
    me_ref, block_ref, owner_ref, levels_ref, weights_ref, *fact_refs = scalars
    live_factors, held_factors, rows, masks, tiles, facts, *counts = scratch
    me = me_ref[0]
    own_factors(live_factors, levels_ref, 1, weights_ref[1, 0])
    held_tables(me, block_ref, fact_refs, facts, held_factors, rows, masks)
    tile_tables(me, owner_ref, others + 1, counts, tiles)
    return live_factors, held_factors, rows, masks, tiles


def start_halo(part, held, live, at, sems):
    copies = [
        pltpu.make_async_copy(part.at[kind], state.at[:, pl.ds(at, DEPTH)], sems.at[kind])
        for kind, state in ((0, held), (1, live))
    ]
    for copy in copies:
        copy.start()
    return copies


def first_half_kernel(others, *refs):
    scalars, refs = refs[: 5 + others], refs[5 + others :]
    before, low, high, send, keep, *refs = refs
    carries, refs = refs[:6], refs[6:]
    held, live, h1, h2, h3, h4, l1, l2, l3, l4, sems, *scratch = refs
    waiting = start_halo(before, held, live, 0, sems)
    for kind, state in ((0, held), (1, live)):
        for number, part in ((1, low), (2, high)):
            copy_layers(part.at[kind], 0, state, number * DEPTH, DEPTH)
    live_factors, held_factors, rows, masks, tiles = half_tables(others, scalars, scratch)
    waiting[0].wait()
    run_sections(held, (h1, h2, h3, h4), HELD_LINES, False, held_factors, False)
    waiting[1].wait()
    run_sections(live, (l1, l2, l3, l4), LIVE_LINES, True, live_factors, False)
    last = ((h1, 8), (h2, 6), (h3, 4), (l1, 8), (l2, 6), (l3, 4))
    for (src, at), out in zip(last, carries):
        copy_layers(src, at, out, 0, 2)
    weigh_and_pack(others, h4, l4, rows, masks, tiles, send, keep)


def second_half_kernel(others, *refs):
    scalars, refs = refs[: 5 + others], refs[5 + others :]
    after, high, _, *refs = refs
    carries, (send, keep, *refs) = refs[:6], refs[6:]
    held, live, h1, h2, h3, h4, l1, l2, l3, l4, sems, *scratch = refs
    waiting = start_halo(after, held, live, DEPTH, sems)
    for kind, state in ((0, held), (1, live)):
        copy_layers(high.at[kind], 0, state, 0, DEPTH)
    for carry, dst in zip(carries, (h1, h2, h3, l1, l2, l3)):
        copy_layers(carry, 0, dst, 0, 2)
    live_factors, held_factors, rows, masks, tiles = half_tables(others, scalars, scratch)
    waiting[0].wait()
    run_sections(held, (h1, h2, h3, h4), HELD_LINES, False, held_factors, True)
    waiting[1].wait()
    run_sections(live, (l1, l2, l3, l4), LIVE_LINES, True, live_factors, True)
    weigh_and_pack(others, h4, l4, rows, masks, tiles, send, keep)


def run_sections(state, stages, lines, wrap, factors, continued):
    for number in range(4):
        row = [factors[number, i] for i in range(17)]
        src = state if number == 0 else stages[number - 1]
        if continued:
            src_at = 3 if number == 0 else 1
            state_at = 3 - number
            dst_at, count = (0 if number == 3 else 2), DEPTH
        else:
            src_at, state_at, dst_at, count = 1, 1 + number, 0, 3 * DEPTH - 2 * (number + 1)
        section(
            src, lines[number], src_at, state, state_at, stages[number], lines[number + 1], dst_at,
            count, row, wrap, number == 3,
        )


def half_step(kernel, scalars, parts, carries_in, layers, last):
    others = len(scalars) - 5
    tiles = scalars[2].shape[1]
    packed = shape(5, DEPTH, 2, 2, ROWS, LANES)
    buffer = lambda count, lines: pltpu.VMEM((5, count, 2, lines, ROWS, LANES), jnp.float32)
    table = lambda *dims, kind=jnp.float32: pltpu.VMEM((*dims, ROWS, LANES), kind)
    carry_shapes = [shape(5, 2, 2, lines, ROWS, LANES) for lines in (6, 8, 10, 4, 4, 4)]
    outs = [packed, packed] + ([] if last else carry_shapes)
    stage_layers = (6, 6, 6, DEPTH) if last else (10, 8, 6, DEPTH)
    return pl.pallas_call(
        functools.partial(kernel, others),
        out_shape=outs,
        in_specs=[spec_smem()] * len(scalars) + [spec_any()] + [spec_vmem()] * (len(parts) - 1 + len(carries_in)),
        out_specs=[spec_vmem()] * len(outs),
        scratch_shapes=[buffer(layers, 4), buffer(layers, 4)]
        + [buffer(count, lines) for count, lines in zip(stage_layers, (6, 8, 10, 12))]
        + [buffer(count, 4) for count in stage_layers]
        + [pltpu.SemaphoreType.DMA((2,))]
        + [table(4, 17), table(4, 17), table(others, 3, kind=jnp.int32), table(others, 3), table(2, 2, kind=jnp.int32)]
        + [pltpu.SMEM((others, 4), jnp.float32)]
        + tile_scratch(others + 1, tiles),
        compiler_params=params(24),
        cost_estimate=cost(8 if last else 12),
        name="second_half" if last else "first_half",
    )(*scalars, *parts, *carries_in)


def after_kernel(count, *refs):
    refs[count][...] = jnp.zeros((ROWS, LANES), jnp.float32)


def there(arrays):
    return pl.pallas_call(
        functools.partial(after_kernel, len(arrays)),
        out_shape=shape(ROWS, LANES),
        in_specs=[spec_any()] * len(arrays),
        out_specs=spec_vmem(),
        compiler_params=params(1),
        cost_estimate=cost(1, 10**12),
        name="there",
    )(*arrays)


def share_kernel(groups, me_ref, owner_ref, keep_low, arrived_low, keep_high, arrived_high, *refs):
    outs, (table, *counts) = refs[:groups], refs[groups:]
    start = counts[0]
    count_tiles(owner_ref, groups, *counts)
    me = me_ref[0]
    for number in range(groups):
        first = first_slot(start[jnp.bitwise_xor(me, number)], me % 2)
        table[number] = jnp.minimum(first + row_index() // 2, ROWS - 1)

    for half, keep, arrived in ((0, keep_low, arrived_low), (1, keep_high, arrived_high)):

        def layer(z, carry, half=half, keep=keep, arrived=arrived):
            odd = row_index() % 2 == 1
            for field in range(5):
                for parity in (0, 1):
                    first = keep[field, z, parity, 0] + arrived[field, z, parity, 0]
                    second = keep[field, z, parity, 1] + arrived[field, z, parity, 1]
                    for number in range(groups):
                        at = table[number]
                        outs[number][field, half * DEPTH + z, parity] = jnp.where(
                            odd, pick_rows(second, at), pick_rows(first, at)
                        )
            return carry

        lax.fori_loop(0, DEPTH, layer, 0)


def share(me, owner, halves, groups):
    piece = shape(5, 2 * DEPTH, 2, ROWS, LANES)
    return pl.pallas_call(
        functools.partial(share_kernel, groups),
        out_shape=[piece] * groups,
        in_specs=[spec_smem()] * 2 + [spec_vmem()] * len(halves),
        out_specs=[spec_vmem()] * groups,
        scratch_shapes=[pltpu.VMEM((groups, ROWS, LANES), jnp.int32)] + tile_scratch(groups, owner.shape[1]),
        compiler_params=params(8),
        cost_estimate=cost(1),
        name="share",
    )(me, owner, *halves)


def collect_kernel(groups, tile_most, me_ref, owner_ref, *rest):
    pieces, (result, out, sems, matrix, *counts) = rest[:groups], rest[groups:]
    pieces = (pieces[0], *pieces[:0:-1])
    count_tiles(owner_ref, groups, *counts)
    one_hot(matrix, True)
    me = me_ref[0]
    mine = counts[1][me]
    swap = counts[0][me] % 2 != me % 2

    def layer(z, carry):
        even = 2 * (row_index() // 2) < mine
        odd = 2 * (row_index() // 2) + 1 < mine
        halves = []
        for parity in (0, 1):
            sums = []
            for kind in (0, 1):
                value = pieces[kind][:, z, parity]
                for other in range(2 + kind, groups, 2):
                    value = value + pieces[other][:, z, parity]
                sums.append(value)
            rows = jnp.concatenate(
                [
                    jnp.where(even, jnp.where(swap, sums[1], sums[0]), 0.0),
                    jnp.where(odd, jnp.where(swap, sums[0], sums[1]), 0.0),
                ]
            )
            halves.append(rows.reshape(10 * ROWS, LANES))
        moved = move_lanes(jnp.concatenate(halves, axis=1), matrix[...]).reshape(2, 5, ROWS, 2 * LANES)
        for kind in (0, 1):
            for field in range(5):
                for slot in range(tile_most // 2):
                    out[2 * slot + kind, field, z] = moved[kind, field, 2 * slot : 2 * slot + 2]
        return carry

    copies = []
    for part in range(4):
        lax.fori_loop(2 * part, 2 * part + 2, layer, 0)
        layers = pl.ds(2 * part, 2)
        copies.append(pltpu.make_async_copy(out.at[:, :, layers], result.at[:, :, layers], sems.at[part]))
        copies[part].start()
    for copy in copies:
        copy.wait()


def collect(me, owner, pieces, tile_most):
    groups = len(pieces)
    dims = (tile_most, 5, 2 * DEPTH, TILE_LINES, 2 * LANES)
    return pl.pallas_call(
        functools.partial(collect_kernel, groups, tile_most),
        out_shape=shape(*dims),
        in_specs=[spec_smem()] * 2 + [spec_vmem()] * len(pieces),
        out_specs=spec_any(),
        scratch_shapes=[pltpu.VMEM(dims, jnp.float32), pltpu.SemaphoreType.DMA((4,)), one_hot_scratch()]
        + tile_scratch(groups, owner.shape[1]),
        compiler_params=params(8),
        cost_estimate=cost(2),
        name="collect",
    )(me, owner, pieces[0], *pieces[:0:-1])


def place_kernel(others, me_ref, block_ref, *rest):
    pieces, (low, high, lines, matrix, table) = rest[:others], rest[others:]
    one_hot(matrix, False)
    me = me_ref[0]
    slots = block_ref.shape[1]
    groups = block_ref.shape[0]
    inner = (me == groups // 2 - 1) | (me == groups // 2)
    for number in range(others):
        for slot in range(HELD_MOST):
            table[number, slot] = -1
        holder = jnp.bitwise_xor(me, min(number + 1, groups - 1))
        rank = jnp.int32(0)
        for slot in range(slots):
            block = block_ref[holder, slot]
            mine = block // slots == me
            if number >= groups - 2:
                mine = mine & (inner if number == groups - 1 else jnp.logical_not(inner))
            table[number, jnp.where(mine, rank, HELD_MOST)] = block % slots
            rank = rank + mine.astype(jnp.int32)
    for number in range(others):
        for slot in range(HELD_MOST):
            block = table[number, slot]

            @pl.when(block >= 0)
            def _(number=number, slot=slot, block=block):
                def copy(z, carry):
                    for field in range(5):
                        for side in (0, 1):
                            lines[z, field, side, pl.ds(block, 4, stride=ROWS), :] = pieces[number][
                                slot, field, z, :, pl.ds(side * LANES, LANES)
                            ]
                    return carry

                lax.fori_loop(0, 2 * DEPTH, copy, 0)

    for half, out in ((0, low), (1, high)):

        def layer(z, carry, half=half, out=out):
            store_lines(lines.at[half * DEPTH + z], matrix, out, z)
            return carry

        lax.fori_loop(0, DEPTH, layer, 0)


def place(me, slot_block, pieces):
    half = shape(5, DEPTH, 2, 4, ROWS, LANES)
    return pl.pallas_call(
        functools.partial(place_kernel, len(pieces)),
        out_shape=[half, half],
        in_specs=[spec_smem()] * 2 + [spec_vmem()] * len(pieces),
        out_specs=[spec_vmem()] * 2,
        scratch_shapes=[
            pltpu.VMEM((2 * DEPTH, 5, 2, 4 * ROWS, LANES), jnp.float32),
            one_hot_scratch(),
            pltpu.SMEM((len(pieces), HELD_MOST + 1), jnp.int32),
        ],
        compiler_params=params(12),
        cost_estimate=cost(3),
        name="place",
    )(me, slot_block, *pieces)


def recover_kernel(levels_ref, before, low, high, after, result, state, s1, s2, s3, s4, out, lines, factors, matrix, sems):
    one_hot(matrix, True)
    own_factors(factors, levels_ref, 0, 1.0)
    for number, part in enumerate((before, low, high, after)):
        copy_layers(part, 0, state, number * DEPTH, DEPTH)
    for number, dst in enumerate((s1, s2, s3, s4)):
        src = state if number == 0 else (s1, s2, s3)[number - 1]
        row = [factors[number, i] for i in range(17)]
        section(src, (0, 4), 1, state, 1 + number, dst, (0, 4), 0, 4 * DEPTH - 2 * (number + 1), row, True, False)

    def layer(z, carry):
        halves = []
        for parity in (0, 1):
            rows = s4[:, z, parity]
            halves.append(jnp.concatenate([rows[:1] + rows[4:], rows[1:]]).reshape(5 * 4 * ROWS, LANES))
        moved = move_lanes(jnp.concatenate(halves, axis=1), matrix[...]).reshape(5, 4, ROWS, 2 * LANES)
        for field in range(5):
            for side in (0, 1):
                for line in range(4):
                    lines[field, side, pl.ds(line, ROWS, stride=4), :] = moved[
                        field, line, :, side * LANES : (side + 1) * LANES
                    ]
                out[field, z, :, pl.ds(side * LANES, LANES)] = lines[field, side]
        pltpu.make_async_copy(out.at[:, z], result.at[:, z], sems.at[z]).start()
        return carry

    lax.fori_loop(0, 2 * DEPTH, layer, 0)
    for z in range(2 * DEPTH):
        pltpu.make_async_copy(out.at[:, z], result.at[:, z], sems.at[z]).wait()


def recover(levels, parts):
    buffer = lambda count: pltpu.VMEM((5, count, 2, 4, ROWS, LANES), jnp.float32)
    return pl.pallas_call(
        recover_kernel,
        out_shape=shape(5, 2 * DEPTH, 4 * ROWS, 2 * LANES),
        in_specs=[spec_smem()] + [spec_vmem()] * 4,
        out_specs=spec_any(),
        scratch_shapes=[buffer(count) for count in (16, 14, 12, 10, 8)]
        + [
            pltpu.VMEM((5, 2 * DEPTH, 4 * ROWS, 2 * LANES), jnp.float32),
            pltpu.VMEM((5, 2, 4 * ROWS, LANES), jnp.float32),
            pltpu.VMEM((4, 17, ROWS, LANES), jnp.float32),
            one_hot_scratch(),
            pltpu.SemaphoreType.DMA((2 * DEPTH,)),
        ],
        compiler_params=params(20),
        cost_estimate=cost(10),
        name="recover",
    )(levels, *parts)


def after_all(*arrays):
    return lax.optimization_barrier(arrays)


def body(checkpoint, slot_block, live_state, levels, coefficients, tile_owner):
    groups = lax.axis_size("buddy")
    slabs = lax.axis_size("slab")
    me = lax.axis_index("buddy").astype(jnp.int32).reshape(1)
    tile_most = 2 * tile_owner.shape[1] // groups
    trade = lambda array, d: lax.ppermute(array, "buddy", [(i, i ^ d) for i in range(groups)])
    upward = lambda array: lax.ppermute(array, "slab", [(i, (i + 1) % slabs) for i in range(slabs)])
    downward = lambda array: lax.ppermute(array, "slab", [((i + 1) % slabs, i) for i in range(slabs)])

    facts = jnp.concatenate([levels.astype(jnp.float32).reshape(-1), coefficients.reshape(-1)])
    other_facts = [trade(facts, d) for d in range(1, groups)]
    high = prepare(1, checkpoint, live_state[0], ())
    before = upward(high)
    sent = gather_slots(me, slot_block, checkpoint, groups - 1)
    sent, other_facts = after_all(sent, other_facts)
    low = prepare(0, checkpoint, live_state[0], other_facts)
    after = downward(low)
    middle = (groups // 2 - 1, groups // 2)
    received = [trade(sent[d - 1], d) for d in range(1, groups - 1)]
    received.append(
        lax.ppermute(sent[-1], "buddy", [(i, i ^ (groups - 1)) for i in range(groups) if i not in middle])
    )

    scalars = (me, slot_block, tile_owner, levels, coefficients, *other_facts)
    send_low, keep_low, *carries = half_step(first_half_kernel, scalars, (before, low, high), (), 3 * DEPTH, False)
    send_low, late, carries[0] = after_all(send_low, sent[-1], carries[0])
    arrived_low = trade(send_low, 1)
    received.append(lax.ppermute(late, "buddy", [middle, middle[::-1]]))
    send_high, keep_high = half_step(second_half_kernel, scalars, (after, high, there(received[:1])), carries, 2 * DEPTH, True)
    arrived_high = trade(send_high, 1)

    keep_high, received = after_all(keep_high, received)
    restored_low, restored_high = place(me, slot_block, received)
    restored_before = upward(restored_high)
    restored_after = downward(restored_low)
    shares = share(me, tile_owner, (keep_low, arrived_low, keep_high, arrived_high), groups)
    pieces = [shares[0]] + [trade(shares[d], d) for d in range(groups - 1, 0, -1)][::-1]
    recovered = recover(levels, (restored_before, restored_low, restored_high, restored_after))
    recovered, pieces[0] = after_all(recovered, pieces[0])
    combined = collect(me, tile_owner, pieces, tile_most)
    return recovered[None], combined


def solution(mesh):
    return jax.shard_map(
        body,
        mesh=mesh,
        in_specs=(
            P("buddy", None, "slab", None, None),
            P(),
            P("buddy", None, "slab", None, None),
            P(None, "buddy", None),
            P(None, "buddy"),
            P("slab", None),
        ),
        out_specs=(P("buddy", None, "slab", None, None), P("buddy", None, "slab", None, None)),
        check_vma=False,
    )
```

```python
import functools

import jax
import jax.numpy as jnp
from jax import lax
from jax.experimental import pallas as pl
from jax.experimental.pallas import tpu as pltpu
from jax.sharding import PartitionSpec as P

VELOCITY = (0.3, -0.2, 0.45)
COURANT = 1.0
TILE_LINES = 2
HELD_MOST = 3
DEPTH = 4
LANES = 128
ROWS = 8


def spec_vmem():
    return pl.BlockSpec(memory_space=pltpu.VMEM)


def spec_smem():
    return pl.BlockSpec(memory_space=pltpu.SMEM)


def spec_any():
    return pl.BlockSpec(memory_space=pl.ANY)


def spec_hbm():
    return pl.BlockSpec(memory_space=pltpu.HBM)


def params(mebibytes):
    return pltpu.CompilerParams(vmem_limit_bytes=mebibytes * 1024 * 1024)


def cost(microseconds, flops=0):
    return pl.CostEstimate(flops=flops, bytes_accessed=microseconds, transcendentals=0)


def shape(*dims):
    return jax.ShapeDtypeStruct(dims, jnp.float32)


def add(*terms):
    total = None
    for term in terms:
        if term is not None:
            total = term if total is None else total + term
    return total


def sub(left, right):
    if right is None:
        return left
    return -right if left is None else left - right


def mul(factor, term):
    return None if term is None else factor * term


def lane_index():
    return lax.broadcasted_iota(jnp.int32, (ROWS, LANES), 1)


def turn_lanes(value, amount):
    return None if value is None else pltpu.roll(value, amount, 1)


def one_hot(out, join):
    row = lax.broadcasted_iota(jnp.int32, out.shape, 0)
    column = lax.broadcasted_iota(jnp.int32, out.shape, 1)
    if join:
        row, column = column, row
    out[...] = (column == row // 2 + LANES * (row % 2)).astype(jnp.float32).astype(jnp.bfloat16)


def move_lanes(rows, matrix):
    top = rows.astype(jnp.bfloat16)
    rest = (rows - top.astype(jnp.float32)).astype(jnp.bfloat16)
    product = lambda part: jnp.dot(part, matrix, preferred_element_type=jnp.float32)
    return product(top) + product(rest)


def one_hot_scratch():
    return pltpu.VMEM((2 * LANES, 2 * LANES), jnp.bfloat16)


def pick_rows(array, at):
    return jnp.take_along_axis(array, at, axis=0)


def direction_factors(axis_number):
    drift = VELOCITY[axis_number]
    wave = abs(drift) + 1.0
    carried = (0.5 * (wave - drift), 0.5 * (wave + drift))
    if drift >= 0:
        rising = (0.0, 0.5 * wave)
        falling = (0.5, 0.5 * drift)
    else:
        rising = (-0.5 * drift, 0.5)
        falling = (0.5 * wave, 0.0)
    return carried, rising, falling


def store_factors(out, spacing, weight):
    waves = [abs(drift) + 1.0 for drift in VELOCITY]
    spread = (waves[0] * spacing[0] + waves[1] * spacing[1]) + waves[2] * spacing[2]
    time_step = COURANT / spread
    for number, part in enumerate((4.0, 3.0, 2.0, 1.0)):
        scale = time_step * (1.0 / part)
        if number == 3:
            scale = scale * weight
        out[number, 0] = -(scale * spread)
        for axis_number in range(3):
            unit = scale * spacing[axis_number]
            carried, rising, falling = direction_factors(axis_number)
            one_sided = rising if 0.0 in rising else falling
            two_sided = falling if 0.0 in rising else rising
            for place, factor in enumerate((*carried, one_sided[0] + one_sided[1], *two_sided)):
                out[number, 1 + 5 * axis_number + place] = unit * factor
        out[number, 16] = weight


def splat(scalar):
    return jnp.full((ROWS, LANES), scalar, jnp.float32)


def spacing_of(level):
    return lax.shift_left(jnp.int32(1), level).astype(jnp.float32)


def own_factors(out, levels_ref, kind, weight):
    store_factors(out, [splat(spacing_of(levels_ref[kind, 0, axis])) for axis in range(3)], splat(weight))


def row_index():
    return lax.broadcasted_iota(jnp.int32, (ROWS, LANES), 0)


def by_slot(scalars):
    value = splat(scalars[0])
    for slot, scalar in enumerate(scalars[1:], 1):
        value = jnp.where(row_index() == slot, scalar, value)
    return value


def held_tables(me, block_ref, fact_refs, facts, factors, rows, masks):
    slots = block_ref.shape[1]
    for number, ref in enumerate(fact_refs):
        for item in range(3):
            facts[number, item] = spacing_of(ref[item].astype(jnp.int32))
        facts[number, 3] = ref[6]
    grids = [block_ref[me, slot] // slots for slot in range(slots)]
    places = [block_ref[me, slot] % slots for slot in range(slots)]
    numbers = [jnp.bitwise_xor(grid, me) - 1 for grid in grids]
    columns = [by_slot([facts[number, item] for number in numbers]) for item in range(4)]
    store_factors(factors, columns[:3], columns[3])
    for other in range(len(fact_refs)):
        for place, shift in enumerate((0, 1, -1)):
            at = jnp.zeros((ROWS, LANES), jnp.int32)
            mask = jnp.zeros((ROWS, LANES), jnp.float32)
            for slot in range(slots):
                target = jnp.where(numbers[slot] == other, (places[slot] + shift) % slots, -1)
                hit = row_index() == target
                at = jnp.where(hit, slot, at)
                mask = jnp.where(hit, 1.0, mask)
            rows[other, place] = at
            masks[other, place] = mask


def count_tiles(owner_ref, groups, start, amount, rank):
    for reader in range(groups):
        amount[reader] = 0
    for tile in range(owner_ref.shape[1]):
        reader = owner_ref[0, tile]
        rank[tile] = amount[reader]
        amount[reader] = amount[reader] + 1
    total = jnp.int32(0)
    for reader in range(groups):
        start[reader] = total
        total = total + amount[reader]


def tile_scratch(groups, tiles):
    return [pltpu.SMEM((groups,), jnp.int32), pltpu.SMEM((groups,), jnp.int32), pltpu.SMEM((tiles,), jnp.int32)]


def first_slot(start, kind):
    return (start + 1 - kind) // 2


def tile_tables(me, owner_ref, groups, counts, table):
    start, amount, rank = counts
    count_tiles(owner_ref, groups, start, amount, rank)
    kind = me % 2
    lists = [[jnp.zeros((ROWS, LANES), jnp.int32) for _ in range(2)] for _ in range(2)]
    for tile in range(owner_ref.shape[1]):
        position = start[owner_ref[0, tile]] + rank[tile]
        for number in (0, 1):
            mine = position % 2 == (kind if number == 1 else 1 - kind)
            hit = row_index() == jnp.where(mine, position // 2, -1)
            lists[number][0] = jnp.where(hit, tile // 2, lists[number][0])
            lists[number][1] = jnp.where(hit, tile % 2, lists[number][1])
    for number in (0, 1):
        for item in (0, 1):
            table[number, item] = lists[number][item]


def acoustic(axis_number, factors, rising_next, rising_prev, falling_next, falling_prev):
    one, two_next, two_prev = factors
    if VELOCITY[axis_number] >= 0:
        rising = mul(one, rising_prev)
        falling = add(mul(two_next, falling_next), mul(two_prev, falling_prev))
    else:
        rising = add(mul(two_next, rising_next), mul(two_prev, rising_prev))
        falling = mul(one, falling_next)
    return add(rising, falling), sub(rising, falling)


def section(src, src_lines, src_at, state, state_at, dst, dst_lines, dst_at, count, factors, wrap, scaled):
    def layer(number, carry):
        cache = {}

        def cell(field, parity, line, step=0):
            low, high = src_lines
            key = (field, parity, line, step)
            if key in cache:
                return cache[key]
            if low <= line < high:
                value = src[field, src_at + number + step, parity, line - low]
            elif wrap and line < low:
                value = pltpu.roll(cell(field, parity, high - 1), 1, 0)
            elif wrap:
                value = pltpu.roll(cell(field, parity, low), ROWS - 1, 0)
            else:
                value = None
            cache[key] = value
            return value

        def pair(axis_number, parity, line, step=0):
            key = ("pair", axis_number, parity, line, step)
            if key not in cache:
                pressure = cell(4, parity, line, step)
                speed = cell(1 + axis_number, parity, line, step)
                cache[key] = (None, None) if pressure is None else (pressure + speed, pressure - speed)
            return cache[key]

        centre = factors[0]
        for line in range(*dst_lines):
            for parity in (0, 1):
                result = [None] * 5
                for field in range(5):
                    terms = mul(centre, cell(field, parity, line))
                    if 0 <= line < 4:
                        held = state[field, state_at + number, parity, line]
                        terms = add(mul(factors[16], held) if scaled else held, terms)
                    result[field] = terms
                for axis_number in range(3):
                    forward, backward, *sound = factors[1 + 5 * axis_number : 6 + 5 * axis_number]

                    def neighbours(read):
                        if axis_number == 0:
                            other = read(1 - parity, line, 0)
                            if parity == 0:
                                return other, [turn_lanes(part, 1) for part in other]
                            return [turn_lanes(part, LANES - 1) for part in other], other
                        if axis_number == 1:
                            return read(parity, line + 1, 0), read(parity, line - 1, 0)
                        return read(parity, line, 1), read(parity, line, -1)

                    for field in range(4):
                        if field != 1 + axis_number:
                            (after,), (before,) = neighbours(
                                lambda *where, field=field: [cell(field, *where)]
                            )
                            result[field] = add(result[field], add(mul(forward, after), mul(backward, before)))
                    after, before = neighbours(lambda *where: pair(axis_number, *where))
                    pressure, speed = acoustic(
                        axis_number, sound, after[0], before[0], after[1], before[1]
                    )
                    result[4] = add(result[4], pressure)
                    result[1 + axis_number] = add(result[1 + axis_number], speed)
                for field in range(5):
                    dst[field, dst_at + number, parity, line - dst_lines[0]] = result[field]
        return carry

    lax.fori_loop(0, count, layer, 0)


def gather_slots_kernel(others, me_ref, block_ref, checkpoint, *outs):
    me = me_ref[0]
    slots = checkpoint.shape[0]
    grids = [block_ref[me, slot] // slots for slot in range(slots)]
    for slot in range(slots):
        rank = jnp.int32(0)
        for earlier in range(slot):
            rank = rank + (grids[earlier] == grids[slot]).astype(jnp.int32)
        for number in range(others):

            @pl.when(grids[slot] == jnp.bitwise_xor(me, number + 1))
            def _(slot=slot, number=number, rank=rank):
                def layer(z, carry):
                    for field in range(5):
                        outs[number][rank, field, z] = checkpoint[slot, field, z]
                    return carry

                lax.fori_loop(0, checkpoint.shape[2], layer, 0)


def gather_slots(me, slot_block, checkpoint, others):
    piece = shape(HELD_MOST, *checkpoint.shape[1:])
    return pl.pallas_call(
        functools.partial(gather_slots_kernel, others),
        out_shape=[piece] * others,
        in_specs=[spec_smem(), spec_smem(), spec_vmem()],
        out_specs=[spec_vmem()] * others,
        compiler_params=params(8),
        cost_estimate=cost(1),
        name="gather_slots",
    )(me, slot_block, checkpoint)


def store_lines(lines, matrix, out, z):
    halves = [lines[:, side].reshape(5 * 4 * ROWS, LANES) for side in (0, 1)]
    moved = move_lanes(jnp.concatenate(halves, axis=1), matrix[...]).reshape(5, 4, ROWS, 2 * LANES)
    for parity in (0, 1):
        lanes = slice(parity * LANES, (parity + 1) * LANES)
        out[0, z, parity] = moved[0, :, :, lanes] - moved[4, :, :, lanes]
        for field in range(1, 5):
            out[field, z, parity] = moved[field, :, :, lanes]


def prepare_kernel(half, firsts, checkpoint, live, *refs):
    out, held_lines, own_lines, matrix = refs[firsts:]
    slots = checkpoint.shape[0]
    one_hot(matrix, False)

    def layer(z, carry):
        for field in range(5):
            for side in (0, 1):
                lanes = pl.ds(side * LANES, LANES)
                for slot in range(slots):
                    held_lines[field, side, pl.ds(slot, 4, stride=ROWS), :] = checkpoint[
                        slot, field, half * DEPTH + z, :, lanes
                    ]
                for group in range(4):
                    rows = live[field, half * DEPTH + z, pl.ds(group * ROWS, ROWS), lanes]
                    for block in (0, 1):
                        own_lines[field, side, pl.ds(2 * group + block, 4, stride=ROWS), :] = rows[
                            4 * block : 4 * block + 4
                        ]
        store_lines(held_lines, matrix, out.at[0], z)
        store_lines(own_lines, matrix, out.at[1], z)
        return carry

    lax.fori_loop(0, DEPTH, layer, 0)


def prepare(half, checkpoint, live, firsts):
    lines = pltpu.VMEM((5, 2, 4 * ROWS, LANES), jnp.float32)
    return pl.pallas_call(
        functools.partial(prepare_kernel, half, len(firsts)),
        out_shape=shape(2, 5, DEPTH, 2, 4, ROWS, LANES),
        in_specs=[spec_vmem(), spec_vmem()] + [spec_any()] * len(firsts),
        out_specs=spec_vmem(),
        scratch_shapes=[lines, lines, one_hot_scratch()],
        compiler_params=params(8),
        cost_estimate=cost(1),
        name="prepare",
    )(checkpoint, live, *firsts)


HELD_LINES = ((0, 4), (-1, 5), (-2, 6), (-3, 7), (-4, 8))
LIVE_LINES = ((0, 4),) * 5
CARRIES = ((0, 6), (0, 8), (0, 10), (1, 4), (1, 4), (1, 4))


def copy_layers(src, src_at, dst, dst_at, count):
    def layer(z, carry):
        dst[:, dst_at + z] = src[:, src_at + z]
        return carry

    lax.fori_loop(0, count, layer, 0)


def weigh_and_pack(others, held_out, live_out, rows_ref, mask_ref, tiles_ref, send, keep):
    def layer(z, carry):
        for field in (4, 0, 1, 2, 3):
            for parity in (0, 1):
                total = [live_out[field, z, parity, line] for line in range(4)]
                for other in range(others):
                    for place, first in ((0, 4), (1, 8), (2, 0)):
                        at = rows_ref[other, place]
                        mask = mask_ref[other, place]
                        for line in range(4):
                            image = held_out[field, z, parity, first + line]
                            total[line] = total[line] + mask * pick_rows(image, at)
                for number, out in ((0, send), (1, keep)):
                    at = tiles_ref[number, 0]
                    lower = tiles_ref[number, 1] == 0
                    for line in (0, 1):
                        value = jnp.where(lower, pick_rows(total[line], at), pick_rows(total[2 + line], at))
                        if field == 0:
                            value = value + out[4, z, parity, line]
                        out[field, z, parity, line] = value
        return carry

    lax.fori_loop(0, DEPTH, layer, 0)


def half_tables(others, scalars, scratch):
    me_ref, block_ref, owner_ref, levels_ref, weights_ref, *fact_refs = scalars
    live_factors, held_factors, rows, masks, tiles, facts, *counts = scratch
    me = me_ref[0]
    own_factors(live_factors, levels_ref, 1, weights_ref[1, 0])
    held_tables(me, block_ref, fact_refs, facts, held_factors, rows, masks)
    tile_tables(me, owner_ref, others + 1, counts, tiles)
    return live_factors, held_factors, rows, masks, tiles


def start_halo(part, held, live, at, sems):
    copies = [
        pltpu.make_async_copy(part.at[kind], state.at[:, pl.ds(at, DEPTH)], sems.at[kind])
        for kind, state in ((0, held), (1, live))
    ]
    for copy in copies:
        copy.start()
    return copies


def first_half_kernel(others, *refs):
    scalars, refs = refs[: 5 + others], refs[5 + others :]
    before, low, high, send, keep, *refs = refs
    carries, refs = refs[:6], refs[6:]
    held, live, h1, h2, h3, h4, l1, l2, l3, l4, sems, *scratch = refs
    waiting = start_halo(before, held, live, 0, sems)
    for kind, state in ((0, held), (1, live)):
        for number, part in ((1, low), (2, high)):
            copy_layers(part.at[kind], 0, state, number * DEPTH, DEPTH)
    live_factors, held_factors, rows, masks, tiles = half_tables(others, scalars, scratch)
    waiting[0].wait()
    run_sections(held, (h1, h2, h3, h4), HELD_LINES, False, held_factors, False)
    waiting[1].wait()
    run_sections(live, (l1, l2, l3, l4), LIVE_LINES, True, live_factors, False)
    last = ((h1, 8), (h2, 6), (h3, 4), (l1, 8), (l2, 6), (l3, 4))
    for (src, at), out in zip(last, carries):
        copy_layers(src, at, out, 0, 2)
    weigh_and_pack(others, h4, l4, rows, masks, tiles, send, keep)


def second_half_kernel(others, *refs):
    scalars, refs = refs[: 5 + others], refs[5 + others :]
    after, high, _, *refs = refs
    carries, (send, keep, *refs) = refs[:6], refs[6:]
    held, live, h1, h2, h3, h4, l1, l2, l3, l4, sems, *scratch = refs
    waiting = start_halo(after, held, live, DEPTH, sems)
    for kind, state in ((0, held), (1, live)):
        copy_layers(high.at[kind], 0, state, 0, DEPTH)
    for carry, dst in zip(carries, (h1, h2, h3, l1, l2, l3)):
        copy_layers(carry, 0, dst, 0, 2)
    live_factors, held_factors, rows, masks, tiles = half_tables(others, scalars, scratch)
    waiting[0].wait()
    run_sections(held, (h1, h2, h3, h4), HELD_LINES, False, held_factors, True)
    waiting[1].wait()
    run_sections(live, (l1, l2, l3, l4), LIVE_LINES, True, live_factors, True)
    weigh_and_pack(others, h4, l4, rows, masks, tiles, send, keep)


def run_sections(state, stages, lines, wrap, factors, continued):
    for number in range(4):
        row = [factors[number, i] for i in range(17)]
        src = state if number == 0 else stages[number - 1]
        if continued:
            src_at = 3 if number == 0 else 1
            state_at = 3 - number
            dst_at, count = (0 if number == 3 else 2), DEPTH
        else:
            src_at, state_at, dst_at, count = 1, 1 + number, 0, 3 * DEPTH - 2 * (number + 1)
        section(
            src, lines[number], src_at, state, state_at, stages[number], lines[number + 1], dst_at,
            count, row, wrap, number == 3,
        )


def half_step(kernel, scalars, parts, carries_in, layers, last):
    others = len(scalars) - 5
    tiles = scalars[2].shape[1]
    packed = shape(5, DEPTH, 2, 2, ROWS, LANES)
    buffer = lambda count, lines: pltpu.VMEM((5, count, 2, lines, ROWS, LANES), jnp.float32)
    table = lambda *dims, kind=jnp.float32: pltpu.VMEM((*dims, ROWS, LANES), kind)
    carry_shapes = [shape(5, 2, 2, lines, ROWS, LANES) for lines in (6, 8, 10, 4, 4, 4)]
    outs = [packed, packed] + ([] if last else carry_shapes)
    stage_layers = (6, 6, 6, DEPTH) if last else (10, 8, 6, DEPTH)
    return pl.pallas_call(
        functools.partial(kernel, others),
        out_shape=outs,
        in_specs=[spec_smem()] * len(scalars) + [spec_any()] + [spec_vmem()] * (len(parts) - 1 + len(carries_in)),
        out_specs=[spec_vmem()] * len(outs),
        scratch_shapes=[buffer(layers, 4), buffer(layers, 4)]
        + [buffer(count, lines) for count, lines in zip(stage_layers, (6, 8, 10, 12))]
        + [buffer(count, 4) for count in stage_layers]
        + [pltpu.SemaphoreType.DMA((2,))]
        + [table(4, 17), table(4, 17), table(others, 3, kind=jnp.int32), table(others, 3), table(2, 2, kind=jnp.int32)]
        + [pltpu.SMEM((others, 4), jnp.float32)]
        + tile_scratch(others + 1, tiles),
        compiler_params=params(24),
        cost_estimate=cost(8 if last else 12),
        name="second_half" if last else "first_half",
    )(*scalars, *parts, *carries_in)


def after_kernel(count, *refs):
    refs[count][...] = jnp.zeros((ROWS, LANES), jnp.float32)


def there(arrays):
    return pl.pallas_call(
        functools.partial(after_kernel, len(arrays)),
        out_shape=shape(ROWS, LANES),
        in_specs=[spec_any()] * len(arrays),
        out_specs=spec_vmem(),
        compiler_params=params(1),
        cost_estimate=cost(1, 10**12),
        name="there",
    )(*arrays)


def share_kernel(groups, me_ref, owner_ref, keep_low, arrived_low, keep_high, arrived_high, *refs):
    outs, (table, *counts) = refs[:groups], refs[groups:]
    start = counts[0]
    count_tiles(owner_ref, groups, *counts)
    me = me_ref[0]
    for number in range(groups):
        first = first_slot(start[jnp.bitwise_xor(me, number)], me % 2)
        table[number] = jnp.minimum(first + row_index() // 2, ROWS - 1)

    for half, keep, arrived in ((0, keep_low, arrived_low), (1, keep_high, arrived_high)):

        def layer(z, carry, half=half, keep=keep, arrived=arrived):
            odd = row_index() % 2 == 1
            for field in range(5):
                for parity in (0, 1):
                    first = keep[field, z, parity, 0] + arrived[field, z, parity, 0]
                    second = keep[field, z, parity, 1] + arrived[field, z, parity, 1]
                    for number in range(groups):
                        at = table[number]
                        outs[number][field, half * DEPTH + z, parity] = jnp.where(
                            odd, pick_rows(second, at), pick_rows(first, at)
                        )
            return carry

        lax.fori_loop(0, DEPTH, layer, 0)


def share(me, owner, halves, groups):
    piece = shape(5, 2 * DEPTH, 2, ROWS, LANES)
    return pl.pallas_call(
        functools.partial(share_kernel, groups),
        out_shape=[piece] * groups,
        in_specs=[spec_smem()] * 2 + [spec_vmem()] * len(halves),
        out_specs=[spec_vmem()] * groups,
        scratch_shapes=[pltpu.VMEM((groups, ROWS, LANES), jnp.int32)] + tile_scratch(groups, owner.shape[1]),
        compiler_params=params(8),
        cost_estimate=cost(1),
        name="share",
    )(me, owner, *halves)


def collect_kernel(groups, tile_most, me_ref, owner_ref, *rest):
    pieces, (result, out, sems, matrix, *counts) = rest[:groups], rest[groups:]
    pieces = (pieces[0], *pieces[:0:-1])
    count_tiles(owner_ref, groups, *counts)
    one_hot(matrix, True)
    me = me_ref[0]
    mine = counts[1][me]
    swap = counts[0][me] % 2 != me % 2

    def layer(z, carry):
        even = 2 * (row_index() // 2) < mine
        odd = 2 * (row_index() // 2) + 1 < mine
        halves = []
        for parity in (0, 1):
            sums = []
            for kind in (0, 1):
                value = pieces[kind][:, z, parity]
                for other in range(2 + kind, groups, 2):
                    value = value + pieces[other][:, z, parity]
                sums.append(value)
            rows = jnp.concatenate(
                [
                    jnp.where(even, jnp.where(swap, sums[1], sums[0]), 0.0),
                    jnp.where(odd, jnp.where(swap, sums[0], sums[1]), 0.0),
                ]
            )
            halves.append(rows.reshape(10 * ROWS, LANES))
        moved = move_lanes(jnp.concatenate(halves, axis=1), matrix[...]).reshape(2, 5, ROWS, 2 * LANES)
        for kind in (0, 1):
            for field in range(5):
                for slot in range(tile_most // 2):
                    out[2 * slot + kind, field, z] = moved[kind, field, 2 * slot : 2 * slot + 2]
        return carry

    copies = []
    for part in range(4):
        lax.fori_loop(2 * part, 2 * part + 2, layer, 0)
        layers = pl.ds(2 * part, 2)
        copies.append(pltpu.make_async_copy(out.at[:, :, layers], result.at[:, :, layers], sems.at[part]))
        copies[part].start()
    for copy in copies:
        copy.wait()


def collect(me, owner, pieces, tile_most):
    groups = len(pieces)
    dims = (tile_most, 5, 2 * DEPTH, TILE_LINES, 2 * LANES)
    return pl.pallas_call(
        functools.partial(collect_kernel, groups, tile_most),
        out_shape=shape(*dims),
        in_specs=[spec_smem()] * 2 + [spec_vmem()] * len(pieces),
        out_specs=spec_any(),
        scratch_shapes=[pltpu.VMEM(dims, jnp.float32), pltpu.SemaphoreType.DMA((4,)), one_hot_scratch()]
        + tile_scratch(groups, owner.shape[1]),
        compiler_params=params(8),
        cost_estimate=cost(2),
        name="collect",
    )(me, owner, pieces[0], *pieces[:0:-1])


def place_kernel(others, me_ref, block_ref, *rest):
    pieces, (low, high, lines, matrix, table) = rest[:others], rest[others:]
    one_hot(matrix, False)
    me = me_ref[0]
    slots = block_ref.shape[1]
    groups = block_ref.shape[0]
    inner = (me == groups // 2 - 1) | (me == groups // 2)
    for number in range(others):
        for slot in range(HELD_MOST):
            table[number, slot] = -1
        holder = jnp.bitwise_xor(me, min(number + 1, groups - 1))
        rank = jnp.int32(0)
        for slot in range(slots):
            block = block_ref[holder, slot]
            mine = block // slots == me
            if number >= groups - 2:
                mine = mine & (inner if number == groups - 1 else jnp.logical_not(inner))
            table[number, jnp.where(mine, rank, HELD_MOST)] = block % slots
            rank = rank + mine.astype(jnp.int32)
    for number in range(others):
        for slot in range(HELD_MOST):
            block = table[number, slot]

            @pl.when(block >= 0)
            def _(number=number, slot=slot, block=block):
                def copy(z, carry):
                    for field in range(5):
                        for side in (0, 1):
                            lines[z, field, side, pl.ds(block, 4, stride=ROWS), :] = pieces[number][
                                slot, field, z, :, pl.ds(side * LANES, LANES)
                            ]
                    return carry

                lax.fori_loop(0, 2 * DEPTH, copy, 0)

    for half, out in ((0, low), (1, high)):

        def layer(z, carry, half=half, out=out):
            store_lines(lines.at[half * DEPTH + z], matrix, out, z)
            return carry

        lax.fori_loop(0, DEPTH, layer, 0)


def place(me, slot_block, pieces):
    half = shape(5, DEPTH, 2, 4, ROWS, LANES)
    return pl.pallas_call(
        functools.partial(place_kernel, len(pieces)),
        out_shape=[half, half],
        in_specs=[spec_smem()] * 2 + [spec_vmem()] * len(pieces),
        out_specs=[spec_vmem()] * 2,
        scratch_shapes=[
            pltpu.VMEM((2 * DEPTH, 5, 2, 4 * ROWS, LANES), jnp.float32),
            one_hot_scratch(),
            pltpu.SMEM((len(pieces), HELD_MOST + 1), jnp.int32),
        ],
        compiler_params=params(12),
        cost_estimate=cost(3),
        name="place",
    )(me, slot_block, *pieces)


def recover_kernel(levels_ref, before, low, high, after, result, state, s1, s2, s3, s4, out, lines, factors, matrix, sems):
    one_hot(matrix, True)
    own_factors(factors, levels_ref, 0, 1.0)
    for number, part in enumerate((before, low, high, after)):
        copy_layers(part, 0, state, number * DEPTH, DEPTH)
    for number, dst in enumerate((s1, s2, s3, s4)):
        src = state if number == 0 else (s1, s2, s3)[number - 1]
        row = [factors[number, i] for i in range(17)]
        section(src, (0, 4), 1, state, 1 + number, dst, (0, 4), 0, 4 * DEPTH - 2 * (number + 1), row, True, False)

    def layer(z, carry):
        halves = []
        for parity in (0, 1):
            rows = s4[:, z, parity]
            halves.append(jnp.concatenate([rows[:1] + rows[4:], rows[1:]]).reshape(5 * 4 * ROWS, LANES))
        moved = move_lanes(jnp.concatenate(halves, axis=1), matrix[...]).reshape(5, 4, ROWS, 2 * LANES)
        for field in range(5):
            for side in (0, 1):
                for line in range(4):
                    lines[field, side, pl.ds(line, ROWS, stride=4), :] = moved[
                        field, line, :, side * LANES : (side + 1) * LANES
                    ]
                out[field, z, :, pl.ds(side * LANES, LANES)] = lines[field, side]
        pltpu.make_async_copy(out.at[:, z], result.at[:, z], sems.at[z]).start()
        return carry

    lax.fori_loop(0, 2 * DEPTH, layer, 0)
    for z in range(2 * DEPTH):
        pltpu.make_async_copy(out.at[:, z], result.at[:, z], sems.at[z]).wait()


def recover(levels, parts):
    buffer = lambda count: pltpu.VMEM((5, count, 2, 4, ROWS, LANES), jnp.float32)
    return pl.pallas_call(
        recover_kernel,
        out_shape=shape(5, 2 * DEPTH, 4 * ROWS, 2 * LANES),
        in_specs=[spec_smem()] + [spec_vmem()] * 4,
        out_specs=spec_any(),
        scratch_shapes=[buffer(count) for count in (16, 14, 12, 10, 8)]
        + [
            pltpu.VMEM((5, 2 * DEPTH, 4 * ROWS, 2 * LANES), jnp.float32),
            pltpu.VMEM((5, 2, 4 * ROWS, LANES), jnp.float32),
            pltpu.VMEM((4, 17, ROWS, LANES), jnp.float32),
            one_hot_scratch(),
            pltpu.SemaphoreType.DMA((2 * DEPTH,)),
        ],
        compiler_params=params(20),
        cost_estimate=cost(10),
        name="recover",
    )(levels, *parts)


def after_all(*arrays):
    return lax.optimization_barrier(arrays)


def body(checkpoint, slot_block, live_state, levels, coefficients, tile_owner):
    groups = lax.axis_size("buddy")
    slabs = lax.axis_size("slab")
    me = lax.axis_index("buddy").astype(jnp.int32).reshape(1)
    tile_most = 2 * tile_owner.shape[1] // groups
    trade = lambda array, d: lax.ppermute(array, "buddy", [(i, i ^ d) for i in range(groups)])
    upward = lambda array: lax.ppermute(array, "slab", [(i, (i + 1) % slabs) for i in range(slabs)])
    downward = lambda array: lax.ppermute(array, "slab", [((i + 1) % slabs, i) for i in range(slabs)])

    facts = jnp.concatenate([levels.astype(jnp.float32).reshape(-1), coefficients.reshape(-1)])
    other_facts = [trade(facts, d) for d in range(1, groups)]
    high = prepare(1, checkpoint, live_state[0], ())
    before = upward(high)
    sent = gather_slots(me, slot_block, checkpoint, groups - 1)
    sent, other_facts = after_all(sent, other_facts)
    low = prepare(0, checkpoint, live_state[0], other_facts)
    after = downward(low)
    middle = (groups // 2 - 1, groups // 2)
    received = [trade(sent[d - 1], d) for d in range(1, groups - 1)]
    received.append(
        lax.ppermute(sent[-1], "buddy", [(i, i ^ (groups - 1)) for i in range(groups) if i not in middle])
    )

    scalars = (me, slot_block, tile_owner, levels, coefficients, *other_facts)
    send_low, keep_low, *carries = half_step(first_half_kernel, scalars, (before, low, high), (), 3 * DEPTH, False)
    send_low, late, carries[0] = after_all(send_low, sent[-1], carries[0])
    arrived_low = trade(send_low, 1)
    received.append(lax.ppermute(late, "buddy", [middle, middle[::-1]]))
    send_high, keep_high = half_step(second_half_kernel, scalars, (after, high, there(received[:1])), carries, 2 * DEPTH, True)
    arrived_high = trade(send_high, 1)

    keep_high, received = after_all(keep_high, received)
    restored_low, restored_high = place(me, slot_block, received)
    restored_before = upward(restored_high)
    restored_after = downward(restored_low)
    shares = share(me, tile_owner, (keep_low, arrived_low, keep_high, arrived_high), groups)
    pieces = [shares[0]] + [trade(shares[d], d) for d in range(groups - 1, 0, -1)][::-1]
    recovered = recover(levels, (restored_before, restored_low, restored_high, restored_after))
    recovered, pieces[0] = after_all(recovered, pieces[0])
    combined = collect(me, tile_owner, pieces, tile_most)
    return recovered[None], combined


def solution(mesh):
    return jax.shard_map(
        body,
        mesh=mesh,
        in_specs=(
            P("buddy", None, "slab", None, None),
            P(),
            P("buddy", None, "slab", None, None),
            P(None, "buddy", None),
            P(None, "buddy"),
            P("slab", None),
        ),
        out_specs=(P("buddy", None, "slab", None, None), P("buddy", None, "slab", None, None)),
        check_vma=False,
    )
```
